256 devices in a mesh: tile: 64 (over x, y_hi, z), slot: 4 (over y_lo, core).
Axes of the slice: x: 4, y: 4 (y_hi: 2, y_lo: 2; y = y_hi * 2 + y_lo), z: 8, core: 2. Of those that a mesh axis runs over, the one named last changes fastest.
Arguments:
- queries: bfloat16 [64, 192, 2560], P('tile', None, 'slot'), may hold values from -5 to 5
- current_keys: bfloat16 [64, 192, 2560], P('tile', None, 'slot'), may hold values from -5 to 5
- current_values: bfloat16 [64, 192, 2560], P('tile', None, 'slot'), may hold values from -5 to 5
- cache_keys: bfloat16 [4, 64, 192, 2560], P('slot', 'tile'), may hold values from -5 to 5
- cache_values: bfloat16 [4, 64, 192, 2560], P('slot', 'tile'), may hold values from -5 to 5
- slot_order: int32 [4], replicated, may hold values from 0 to 3, each once
- tile_mask: int32 [64, 9], P('tile'), may hold values 0 or 1
- window_reach: int32 [64, 2], P('tile'), may hold values from 1 to 4
Outputs:
- attended: bfloat16 [64, 192, 2560], P('tile', None, 'slot')
The draws below stay inside these ranges and needn't reach their ends.
Inputs may be any that keep to these rules, and one draw needn't show every extreme that they name: slot_order[c] is the age of the stretch in slot c, 0 the most recent; each age once.
All inputs are finite; a program needn't handle non-finite values. No bound on the sum of `tile_mask` on one device may be relied on, other than what follows from the above.
Results may differ from the reference program's by a relative error of at most 0.0072.
Values may be sent and summed in bfloat16 or wider, within the bound.
A program may use at most 128 MiB of HBM per device.

```python
import math
import jax
import jax.numpy as jnp
from jax import lax

TH = 8
TW = 8
F = 3
HALO = 4
GX = 8
HEADS = 20
HD = 128
PAIRS = 22
STRETCHES = 4
GY = 8
TOKT = 192
KEYS = 768
N_TILE = 64


def draw_queries(key, part):
    key = jax.random.fold_in(key, 11)
    return jnp.clip(1.6 * jax.random.normal(key, (N_TILE, TOKT, HEADS * HD), jnp.float32), -5.0, 5.0).astype(jnp.bfloat16)


def draw_current_keys(key, part):
    key = jax.random.fold_in(key, 12)
    return jnp.clip(1.6 * jax.random.normal(key, (N_TILE, TOKT, HEADS * HD), jnp.float32), -5.0, 5.0).astype(jnp.bfloat16)


def draw_window_reach(key, part):
    key = jax.random.fold_in(key, 21)
    reaches = jax.random.randint(key, (N_TILE, 2), 1, HALO + 1)
    highest = jax.random.randint(jax.random.fold_in(key, 1), (2,), 0, N_TILE)
    lowest = jax.random.randint(jax.random.fold_in(key, 2), (2,), 0, N_TILE)
    tiles = jnp.arange(N_TILE)[:, None]
    reaches = jnp.where(tiles == highest[None, :], HALO, reaches)
    reaches = jnp.where((tiles == lowest[None, :]) & (tiles != highest[None, :]), 1, reaches)
    return reaches.astype(jnp.int32)


def with_ends(drawn, key, smallest, largest):
    shape = drawn.shape
    index_at = [jax.random.randint(jax.random.fold_in(key, axis), (), 0, shape[axis]) for axis in range(len(shape))]
    drawn = drawn.at[tuple(index_at)].set(smallest)
    longest = shape.index(max(shape))
    index_at[longest] = (index_at[longest] + 1) % shape[longest]
    return drawn.at[tuple(index_at)].set(largest)


def shard_levels(key, shape, shards, smallest, largest):
    factor_of = 1.0
    for axis_at, blocks in shards:
        heights = jax.random.uniform(jax.random.fold_in(jax.random.fold_in(key, 6), axis_at), (blocks,), jnp.float32, smallest / len(shards), largest / len(shards))
        factor_of = factor_of * jnp.repeat(jnp.exp(heights), shape[axis_at] // blocks).reshape((-1,) + (1,) * (len(shape) - 1 - axis_at))
    return factor_of


def scatter_about(rng, extent, deviation, bound, shards=(), held_as=jnp.bfloat16):
    array = jax.random.normal(rng, extent, jnp.float32) * deviation
    if len(shards) > 0:
        array = shard_levels(rng, extent, shards, -0.22, 0.18) * array
    return jnp.clip(array, min=-bound, max=bound).astype(held_as)


def setup_inputs(seed: int = 0) -> dict:
    key_of = jax.random.split(jax.random.key(seed), 9)
    return {
        "queries": draw_queries(jax.random.fold_in(key_of[8], 71), 0),
        "current_keys": draw_current_keys(jax.random.fold_in(key_of[8], 71), 0),
        "current_values": scatter_about(key_of[2], (N_TILE, TOKT, HEADS * HD), 1.0, 5.0, ((0, 64), (2, 4))),
        "cache_keys": scatter_about(key_of[3], (STRETCHES, N_TILE, TOKT, HEADS * HD), 1.6, 5.0, ((0, 4), (1, 64))),
        "cache_values": scatter_about(key_of[4], (STRETCHES, N_TILE, TOKT, HEADS * HD), 1.0, 5.0, ((0, 4), (1, 64))),
        "slot_order": jax.random.permutation(key_of[5], STRETCHES).astype(jnp.int32),
        "tile_mask": with_ends((jax.random.randint(key_of[6], (N_TILE, 9), 0, 2) < 1).astype(jnp.int32), jax.random.fold_in(key_of[6], 1), 0, 1),
        "window_reach": draw_window_reach(jax.random.fold_in(key_of[8], 71), 0),
    }


def rotate_pairs(matrix, moments):
    heads_count = matrix.shape[-1] // HD
    shaped = matrix.reshape(matrix.shape[:-1] + (heads_count, HD))
    frequency = 10000.0 ** (-jnp.arange(PAIRS, dtype=jnp.float32) / PAIRS)
    angles = moments[..., None, None] * frequency
    cosine = jnp.cos(angles)
    sine = jnp.sin(angles)
    first_half = shaped[..., :PAIRS]
    second_half = shaped[..., PAIRS:2 * PAIRS]
    turned = jnp.concatenate([first_half * cosine - second_half * sine, first_half * sine + second_half * cosine, shaped[..., 2 * PAIRS:]], axis=-1)
    return turned.reshape(matrix.shape)

def window_mask(row_tile, col_tile, rows_tiles, bits, reach_rows, reach_cols):
    extent_rows = jnp.arange(TH + 2 * HALO, dtype=jnp.int32)
    offset_rows = extent_rows - HALO
    step_rows = jnp.where(extent_rows < HALO, -1, jnp.where(extent_rows >= TH + HALO, 1, 0))
    rows_good = (offset_rows >= -reach_rows) & (offset_rows < TH + reach_rows) & (row_tile + step_rows >= 0) & (row_tile + step_rows < rows_tiles)
    extent_cols = jnp.arange(TW + 2 * HALO, dtype=jnp.int32)
    offset_cols = extent_cols - HALO
    step_cols = jnp.where(extent_cols < HALO, -1, jnp.where(extent_cols >= TW + HALO, 1, 0))
    cols_good = (offset_cols >= -reach_cols) & (offset_cols < TW + reach_cols) & (col_tile + step_cols >= 0) & (col_tile + step_cols < GX)
    neighbour = (step_rows[:, None] + 1) * 3 + (step_cols[None, :] + 1)
    indices = jnp.arange(9, dtype=jnp.int32)
    forced = jnp.where(indices == 4, 1, bits)
    chosen = lax.optimization_barrier(jnp.sum(jnp.where(neighbour[..., None] == indices, forced, 0), axis=-1))
    grid_good = rows_good[:, None] & cols_good[None, :] & (chosen > 0)
    return jnp.broadcast_to(grid_good, (F,) + grid_good.shape).reshape(-1)

def attend_blocks(rotated, block_keys, block_values, allowed):
    scaling = 1.0 / math.sqrt(HD)
    for number in range(block_keys.shape[0]):
        scores = jnp.einsum('qhd,khd->hqk', rotated.astype(jnp.float32), block_keys[number].astype(jnp.float32)) * scaling
        scores = jnp.where(allowed, scores, -jnp.inf)
        highest = lax.optimization_barrier(jnp.max(scores, axis=-1))
        if number == 0:
            newest = highest
        else:
            newest = jnp.maximum(running, highest)
        weights = jnp.exp(scores - newest[..., None]).astype(jnp.bfloat16)
        product = jnp.einsum('hqk,khd->hqd', weights.astype(jnp.float32), block_values[number].astype(jnp.float32))
        partial_total = lax.optimization_barrier(jnp.sum(weights.astype(jnp.float32), axis=-1))
        if number == 0:
            total = partial_total
            summed = product
        else:
            factor = jnp.exp(running - newest)
            total = total * factor + partial_total
            summed = summed * factor[..., None] + product
        running = newest
    result = summed / total[..., None]
    return jnp.transpose(result, (1, 0, 2)).reshape(rotated.shape[0], -1).astype(jnp.bfloat16)

def to_grid(stacked):
    count = stacked.shape[0]
    shaped = stacked.reshape(count, GY, GX, F, TH, TW, stacked.shape[-1])
    shaped = jnp.transpose(shaped, (0, 3, 1, 4, 2, 5, 6)).reshape(count, F, GY * TH, GX * TW, stacked.shape[-1])
    return jnp.pad(shaped, ((0, 0), (0, 0), (HALO, HALO), (HALO, HALO), (0, 0)))

def reference(queries, current_keys, current_values, cache_keys, cache_values, slot_order, tile_mask, window_reach):
    frames = jnp.arange(TOKT, dtype=jnp.int32) // (TH * TW)
    present = (STRETCHES * F + frames).astype(jnp.float32)
    rotated = rotate_pairs(queries.astype(jnp.float32), present).astype(jnp.bfloat16)
    keys_list = [rotate_pairs(current_keys.astype(jnp.float32), present).astype(jnp.bfloat16)]
    for number in range(STRETCHES):
        moments = ((STRETCHES - 1 - slot_order[number]) * F + frames).astype(jnp.float32)
        keys_list.append(rotate_pairs(cache_keys[number].astype(jnp.float32), moments).astype(jnp.bfloat16))
    values_list = [current_values] + [cache_values[number] for number in range(STRETCHES)]
    padded_keys = to_grid(jnp.stack(keys_list))
    padded_values = to_grid(jnp.stack(values_list))
    window_shape = (STRETCHES + 1, F, TH + 2 * HALO, TW + 2 * HALO, HEADS * HD)

    def per_tile(inputs):
        tile_id, tile_queries, bits, reach_pair = inputs
        row_tile = (tile_id // GX).astype(jnp.int32)
        col_tile = (tile_id % GX).astype(jnp.int32)
        zero = jnp.zeros((), jnp.int32)
        starts = (zero, zero, (row_tile * TH).astype(jnp.int32), (col_tile * TW).astype(jnp.int32), zero)
        window_keys = lax.dynamic_slice(padded_keys, starts, window_shape).reshape(STRETCHES + 1, KEYS, HEADS, HD)
        window_values = lax.dynamic_slice(padded_values, starts, window_shape).reshape(STRETCHES + 1, KEYS, HEADS, HD)
        allowed = window_mask(row_tile, col_tile, GY, bits, reach_pair[0], reach_pair[1])
        return attend_blocks(tile_queries.reshape(TOKT, HEADS, HD), window_keys, window_values, allowed)
    return lax.map(per_tile, (jnp.arange(N_TILE, dtype=jnp.int32), rotated, tile_mask, window_reach))
```

```python
import functools
import math

import jax
import jax.numpy as jnp
from jax import lax
from jax.experimental import pallas as pl
from jax.experimental.pallas import tpu as pltpu
from jax.sharding import PartitionSpec as P

TH = 8
TW = 8
F = 3
HALO = 4
GX = 8
HD = 128
PAIRS = 22
TOKT = 192
STRETCHES = 4
HALF = 48
ROUNDS = 5
GROUPS = 4
BLOCKS = GROUPS + 1
NEGATIVE = -1e30
SCALE = math.log2(math.e) / math.sqrt(HD)
MESH = pl.DeviceIdType.MESH
O, U, D = 0, 1, 2
(
    Z_RIGHT,
    Z_LEFT,
    Q_CHIP,
    Q_UP,
    Q_DOWN,
    Q_PASS,
    Q_CORE0,
    Q_CORE2,
    P_CORE,
    L_CORE,
    P_CHIP,
    L_CHIP,
    P_UP,
    L_UP,
    P_DOWN,
    L_DOWN,
    MESSAGES,
) = range(17)


def nt_dot(a, b):
    return lax.dot_general(a, b, (((1,), (1,)), ((), ())), preferred_element_type=jnp.float32)


def dot(a, b):
    return lax.dot_general(a, b, (((1,), (0,)), ((), ())), preferred_element_type=jnp.float32)


def iota(shape, dim):
    return lax.broadcasted_iota(jnp.int32, shape, dim)


def spread(rows):
    padded = jnp.concatenate([rows, jnp.zeros((HD - rows.shape[0], 256), jnp.float32)], axis=0)
    return padded.T[:TOKT]


def gathered(columns):
    padded = jnp.concatenate([columns, jnp.zeros((256 - TOKT, HD), jnp.float32)], axis=0)
    return padded.T[:8]


def kernel(
    grid_rows,
    order_ref,
    mask_ref,
    reach_ref,
    q_hbm,
    k_hbm,
    v_hbm,
    ck_hbm,
    cv_hbm,
    out_ref,
    q_in,
    k_in,
    v_in,
    ck_in,
    cv_in,
    kv,
    q,
    par,
    par_up,
    par_down,
    bias,
    table,
    part,
    lse,
    p1_send,
    p1_recv,
    l1_send,
    l1_recv,
    p2_keep,
    p2_send,
    p2_recv,
    l2_keep,
    l2_send,
    l2_recv,
    p3_keep,
    p3_send,
    p3_recv,
    l3_keep,
    l3_recv,
    in_sem,
    par_send_sem,
    par_recv_sem,
    send_sem,
    recv_sem,
):
    tile = lax.axis_index("tile")
    slot = lax.axis_index("slot")
    row, col = tile // GX, lax.rem(tile, GX)
    tiles = grid_rows * GX
    core_slot = slot + 1 - 2 * lax.rem(slot, 2)
    chip_slot = lax.rem(slot + 2, 4)
    right = row * GX + lax.rem(col + 1, GX)
    left = row * GX + lax.rem(col + GX - 1, GX)
    up = lax.rem(tile + tiles - GX, tiles)
    down = lax.rem(tile + GX, tiles)
    core_mate, chip_mate = (tile, core_slot), (tile, chip_slot)
    at_right, at_left = (right, slot), (left, slot)
    at_up, at_down = (up, chip_slot), (down, chip_slot)

    inputs = [
        pltpu.make_async_copy(source, target, in_sem.at[n])
        for n, (source, target) in enumerate(
            ((ck_hbm, ck_in), (cv_hbm, cv_in), (k_hbm, k_in), (v_hbm, v_in), (q_hbm, q_in))
        )
    ]
    for copy in inputs:
        copy.start()

    barrier = pltpu.get_barrier_semaphore()
    partners = (core_mate, chip_mate, at_right, at_left, at_up, at_down)
    for partner in partners:
        pl.semaphore_signal(barrier, inc=1, device_id=partner, device_id_type=MESH)

    def message(number, h, source, target, device):
        return pltpu.make_async_remote_copy(
            src_ref=source,
            dst_ref=target,
            send_sem=send_sem.at[number, h],
            recv_sem=recv_sem.at[number, h],
            device_id=device,
            device_id_type=MESH,
        )

    messages = {
        Z_RIGHT: lambda h: message(Z_RIGHT, h, kv.at[h, 2], kv.at[h, 0], at_right),
        Z_LEFT: lambda h: message(Z_LEFT, h, kv.at[h, 1], kv.at[h, 3], at_left),
        Q_CHIP: lambda h: message(Q_CHIP, h, q.at[h, 0, O], q.at[h, 2, O], chip_mate),
        Q_UP: lambda h: message(Q_UP, h, q.at[h, 0, O], q.at[h, 2, D], at_up),
        Q_DOWN: lambda h: message(Q_DOWN, h, q.at[h, 0, O], q.at[h, 2, U], at_down),
        Q_PASS: lambda h: message(
            Q_PASS, h, q.at[h, 2, pl.ds(U, 2)], q.at[h, 0, pl.ds(U, 2)], chip_mate
        ),
        Q_CORE0: lambda h: message(Q_CORE0, h, q.at[h, 0], q.at[h, 1], core_mate),
        Q_CORE2: lambda h: message(Q_CORE2, h, q.at[h, 2], q.at[h, 3], core_mate),
        P_CORE: lambda h: message(P_CORE, h, p1_send.at[h], p1_recv.at[h], core_mate),
        L_CORE: lambda h: message(L_CORE, h, l1_send.at[h], l1_recv.at[h], core_mate),
        P_CHIP: lambda h: message(P_CHIP, h, p2_send.at[h], p2_recv.at[h], chip_mate),
        L_CHIP: lambda h: message(L_CHIP, h, l2_send.at[h], l2_recv.at[h], chip_mate),
        P_UP: lambda h: message(P_UP, h, p3_send.at[h, 0], p3_recv.at[h, 0], at_up),
        L_UP: lambda h: message(L_UP, h, l3_keep.at[h], l3_recv.at[h, 0], at_up),
        P_DOWN: lambda h: message(P_DOWN, h, p3_send.at[h, 1], p3_recv.at[h, 1], at_down),
        L_DOWN: lambda h: message(L_DOWN, h, l3_keep.at[h], l3_recv.at[h, 1], at_down),
    }

    def start(h, *numbers):
        for number in numbers:
            messages[number](h).start()

    def arrived(h, *numbers):
        for number in numbers:
            messages[number](h).wait_recv()

    age = jnp.int32(0)
    for n in range(STRETCHES):
        age = age + jnp.where(slot == n, order_ref[n], 0)
    sub, lane = iota((8, HD), 0), iota((8, HD), 1)
    moment = jnp.where(sub < F, (STRETCHES - 1 - age) * F + sub, STRETCHES * F + sub - F)
    pair = jnp.where(lane < PAIRS, lane, lane - PAIRS).astype(jnp.float32)
    frequency = jnp.exp(pair * (-math.log(10000.0) / PAIRS))
    angle = jnp.where(lane < 2 * PAIRS, moment.astype(jnp.float32) * frequency, 0.0)
    cosine, sine = jnp.cos(angle), jnp.sin(angle)
    for n in range(2):
        for f in range(F):
            for at, values in ((0, cosine), (1, sine)):
                wanted = jnp.broadcast_to(values[n * F + f : n * F + f + 1], (16, HD))
                for quarter in range(4):
                    table[n, at, pl.ds(quarter * HALF + f * 16, 16)] = wanted
                if n == 1:
                    for part_at in range(4):
                        table[2, at, pl.ds(f * 64 + part_at * 16, 16)] = wanted

    first, second = iota((HD, HD), 0), iota((HD, HD), 1)
    exchange = jnp.where(
        (second < PAIRS) & (first == second + PAIRS),
        -1.0,
        jnp.where((second >= PAIRS) & (second < 2 * PAIRS) & (first == second - PAIRS), 1.0, 0.0),
    ).astype(jnp.bfloat16)
    at = iota((TOKT, TOKT), 0)
    side = (at >= 2 * HALF).astype(jnp.int32)
    rest = at - side * 2 * HALF
    lower = (rest >= HALF).astype(jnp.int32)
    rest = rest - lower * HALF
    source = (
        (rest >> 4) * TH * TW + (lower * HALO + ((rest >> 2) & 3)) * TW + side * HALO + (rest & 3)
    )
    quarters = (iota((TOKT, TOKT), 1) == source).astype(jnp.float32).astype(jnp.bfloat16)

    def turned(x, n):
        swapped = dot(x.astype(jnp.bfloat16), exchange)
        return x.astype(jnp.float32) * table[n, 0] + swapped * table[n, 1]

    def group_of(e):
        if e == 0:
            return slot
        if e == 1:
            return core_slot
        if e == 2:
            return chip_slot
        return 3 - slot

    def prepare_block(h, e, keys, values, n):
        both = dot(quarters, jnp.concatenate([keys, values], axis=1))
        new_keys = turned(both[:, :HD], n).astype(jnp.bfloat16)
        new_values = both[:, HD:].astype(jnp.bfloat16)
        for g in range(2):
            for lower_half in range(2):
                at_row = (g * 2 + lower_half) * HALF
                kv[h, 1 + g, 0, e, lower_half] = new_keys[at_row : at_row + HALF]
                kv[h, 1 + g, 1, e, lower_half] = new_values[at_row : at_row + HALF]

    def prepare(h):
        for e in range(GROUPS):
            lanes = pl.ds(pl.multiple_of((group_of(e) * ROUNDS + h) * HD, HD), HD)
            prepare_block(h, e, ck_in[0, 0, :, lanes], cv_in[0, 0, :, lanes], 0)
        lanes = pl.ds(pl.multiple_of(h * HD, HD), HD)
        prepare_block(h, GROUPS, k_in[0, :, lanes], v_in[0, :, lanes], 1)
        q[h, 0, O] = turned(q_in[0, :, lanes], 2).astype(jnp.bfloat16)

    entry = iota((16, HD), 0)
    block = jnp.zeros((16, HD), jnp.int32)
    for n in range(9):
        block = jnp.where(entry == n, mask_ref[0, n], block)
    for n in range(2):
        block = jnp.where(entry == 9 + n, reach_ref[0, n], block)
    par[...] = block

    for copy in inputs:
        copy.wait()
    pl.semaphore_wait(barrier, len(partners))

    par_copies = [
        pltpu.make_async_remote_copy(
            src_ref=par,
            dst_ref=target,
            send_sem=par_send_sem.at[n],
            recv_sem=par_recv_sem.at[n],
            device_id=device,
            device_id_type=MESH,
        )
        for n, (target, device) in enumerate(((par_up, at_down), (par_down, at_up)))
    ]
    for copy in par_copies:
        copy.start()

    def first_sends(h, carry):
        prepare(h)
        start(h, Z_RIGHT, Z_LEFT, Q_UP, Q_DOWN, Q_CHIP)
        return carry

    lax.fori_loop(0, ROUNDS, first_sends, 0)

    for copy in par_copies:
        copy.wait_recv()

    key, feature = iota((TOKT, HD), 0), iota((TOKT, HD), 1)
    from_left, from_right = key < HALF, key >= 3 * HALF
    key_row, key_col = (key >> 2) & 3, key & 3

    def window(values, dy, rows_good):
        bits = [values[(dy + 1) * 3 + n : (dy + 1) * 3 + n + 1] for n in range(3)]
        reach_cols = values[10:11]
        middle = jnp.full((1, HD), 1, jnp.int32) if dy == 0 else bits[1]
        on_left = from_left & (key_col >= HALO - reach_cols) & (bits[0] > 0) & (col >= 1)
        on_right = from_right & (key_col < reach_cols) & (bits[2] > 0) & (col < GX - 1)
        inside = (key >= HALF) & (key < 3 * HALF) & (middle > 0)
        good = (on_left | on_right | inside) & rows_good
        return jnp.where(good, 0.0, NEGATIVE)

    above, below, here = par_up[...], par_down[...], par[...]
    own_window = window(here, 0, key >= 0)
    up_window = window(above, 1, (key_row < above[9:10]) & (row >= 1))
    down_window = window(below, -1, (key_row >= HALO - below[9:10]) & (row < grid_rows - 1))
    for n, other in enumerate((up_window, down_window)):
        bias[n] = jnp.where(
            feature == 0, other, jnp.where(feature == 1, own_window, 0.0)
        ).astype(jnp.bfloat16)

    def pass_on(h):
        arrived(h, Q_UP, Q_DOWN)
        start(h, Q_PASS)

    def share(h):
        arrived(h, Q_CHIP)
        start(h, Q_CORE2)
        arrived(h, Q_PASS)
        start(h, Q_CORE0)

    def attend(queries, marker, keys, values):
        scores = nt_dot(jnp.concatenate([queries, marker], axis=1), keys)
        highest = jnp.max(scores, axis=1, keepdims=True)
        weights = jnp.exp2((scores - highest) * SCALE).astype(jnp.bfloat16)
        summed = dot(weights, values)
        total = summed[:, HD:]
        return summed[:, :HD] / total, highest * SCALE + jnp.log2(total)

    def compute(h):
        other_marker = jnp.where(feature == 0, 1.0, 0.0).astype(jnp.bfloat16)
        own_marker = jnp.where(feature == 1, 1.0, 0.0).astype(jnp.bfloat16)
        ones = jnp.ones((TOKT, HD), jnp.bfloat16)
        kept = jnp.zeros((TOKT, HD), jnp.float32)
        sent = jnp.zeros((TOKT, HD), jnp.float32)
        for e in range(GROUPS):
            keys, values = [[], []], [[], []]
            for block_at in (e,) if e > 0 else (0, GROUPS):
                for lower_half in range(2):
                    these_keys = kv[h, :, 0, block_at, lower_half].reshape(TOKT, HD)
                    these_values = kv[h, :, 1, block_at, lower_half].reshape(TOKT, HD)
                    keys[lower_half].append(
                        jnp.concatenate([these_keys, bias[lower_half]], axis=1)
                    )
                    values[lower_half].append(jnp.concatenate([these_values, ones], axis=1))
            for tile_kind, halves, marker in (
                (U, (0,), other_marker),
                (D, (1,), other_marker),
                (O, (0, 1), own_marker),
            ):
                all_keys = jnp.concatenate([x for n in halves for x in keys[n]], axis=0)
                all_values = jnp.concatenate([x for n in halves for x in values[n]], axis=0)
                result, level = attend(q[h, e, tile_kind], marker, all_keys, all_values)
                place = e // 2 * 3 + tile_kind
                if e % 2 == 0:
                    part[e // 2, tile_kind] = result
                    kept = jnp.where(feature == place, level, kept)
                else:
                    p1_send[h, e // 2, tile_kind] = result.astype(jnp.bfloat16)
                    sent = jnp.where(feature == place, level, sent)
        lse[...] = kept
        l1_send[h] = sent
        start(h, P_CORE, L_CORE)

    def after_core(h):
        arrived(h, P_CORE, L_CORE)
        mine, theirs = lse[...], l1_recv[h]
        newest = jnp.maximum(mine, theirs)
        mine_part, theirs_part = jnp.exp2(mine - newest), jnp.exp2(theirs - newest)
        total = mine_part + theirs_part
        mine_part, theirs_part = mine_part / total, theirs_part / total
        rows = gathered(newest + jnp.log2(total))
        for tile_kind in range(3):
            for n in range(2):
                place = n * 3 + tile_kind
                result = (
                    part[n, tile_kind] * mine_part[:, place : place + 1]
                    + p1_recv[h, n, tile_kind].astype(jnp.float32)
                    * theirs_part[:, place : place + 1]
                )
                if (n == 0) == (tile_kind == O):
                    p2_keep[h, tile_kind] = result
                else:
                    p2_send[h, tile_kind] = result.astype(jnp.bfloat16)
        start(h, P_CHIP)
        l2_keep[h] = rows
        l2_send[h] = jnp.concatenate(
            [rows[3:4], rows[0:1], rows[0:1], rows[0:1], rows[1:2], rows[2:3], rows[0:2]], axis=0
        )
        start(h, L_CHIP)

    def after_chip(h):
        arrived(h, P_CHIP, L_CHIP)
        mine, theirs = l2_keep[h], l2_recv[h]
        newest = jnp.maximum(mine, theirs)
        mine_part, theirs_part = jnp.exp2(mine - newest), jnp.exp2(theirs - newest)
        total = mine_part + theirs_part
        l3_keep[h] = newest + jnp.log2(total)
        start(h, L_UP, L_DOWN)
        columns = spread(jnp.concatenate([mine_part / total, theirs_part / total], axis=0))
        for tile_kind, place in ((U, 4), (D, 5), (O, 0)):
            result = (
                p2_keep[h, tile_kind] * columns[:, place : place + 1]
                + p2_recv[h, tile_kind].astype(jnp.float32) * columns[:, 8 + place : 9 + place]
            )
            if tile_kind == O:
                p3_keep[h] = result
            else:
                p3_send[h, tile_kind - 1] = result.astype(jnp.bfloat16)
                start(h, P_UP if tile_kind == U else P_DOWN)

    def after_row(h):
        arrived(h, P_UP, L_UP, P_DOWN, L_DOWN)
        own = l3_keep[h][0:1]
        from_down = l3_recv[h, 0][4:5]
        from_up = l3_recv[h, 1][5:6]
        newest = jnp.maximum(jnp.maximum(own, from_down), from_up)
        parts = [jnp.exp2(x - newest) for x in (own, from_down, from_up)]
        total = parts[0] + parts[1] + parts[2]
        columns = spread(
            jnp.concatenate(
                [x / total for x in parts] + [jnp.zeros((5, 256), jnp.float32)], axis=0
            )
        )
        result = (
            p3_keep[h] * columns[:, 0:1]
            + p3_recv[h, 0].astype(jnp.float32) * columns[:, 1:2]
            + p3_recv[h, 1].astype(jnp.float32) * columns[:, 2:3]
        )
        lanes = pl.ds(pl.multiple_of(h * HD, HD), HD)
        out_ref[0, :, lanes] = result.astype(jnp.bfloat16)

    pass_on(0)
    share(0)

    def step(i, carry):
        @pl.when(i + 1 < ROUNDS)
        def _():
            pass_on(i + 1)

        @pl.when((i >= 1) & (i <= ROUNDS))
        def _():
            after_core(i - 1)

        @pl.when((i >= 2) & (i <= ROUNDS + 1))
        def _():
            after_chip(i - 2)

        @pl.when(i >= 3)
        def _():
            after_row(i - 3)

        @pl.when(i + 1 < ROUNDS)
        def _():
            share(i + 1)

        @pl.when(i < ROUNDS)
        def _():
            arrived(i, Q_CORE0, Q_CORE2, Z_RIGHT, Z_LEFT)
            compute(i)

        return carry

    lax.fori_loop(0, ROUNDS + 3, step, 0)

    def finish(h, carry):
        for number in range(MESSAGES):
            messages[number](h).wait_send()
        return carry

    lax.fori_loop(0, ROUNDS, finish, 0)
    for copy in par_copies:
        copy.wait_send()


def solution(mesh):
    grid_rows = mesh.shape["tile"] // GX
    bf16, f32, i32 = jnp.bfloat16, jnp.float32, jnp.int32
    wide = GROUPS * ROUNDS * HD

    def on_device(queries, keys, values, cache_keys, cache_values, order, tile_mask, reach):
        smem = pl.BlockSpec(memory_space=pltpu.SMEM)
        anywhere = pl.BlockSpec(memory_space=pl.ANY)
        piece = (TOKT, HD)
        return pl.pallas_call(
            functools.partial(kernel, grid_rows),
            out_shape=jax.ShapeDtypeStruct((1, TOKT, ROUNDS * HD), bf16),
            in_specs=[smem] * 3 + [anywhere] * 5,
            out_specs=pl.BlockSpec(memory_space=pltpu.VMEM),
            scratch_shapes=[
                pltpu.VMEM((1, TOKT, ROUNDS * HD), bf16),
                pltpu.VMEM((1, TOKT, ROUNDS * HD), bf16),
                pltpu.VMEM((1, TOKT, ROUNDS * HD), bf16),
                pltpu.VMEM((1, 1, TOKT, wide), bf16),
                pltpu.VMEM((1, 1, TOKT, wide), bf16),
                pltpu.VMEM((ROUNDS, 4, 2, BLOCKS, 2, HALF, HD), bf16),
                pltpu.VMEM((ROUNDS, GROUPS, 3) + piece, bf16),
                pltpu.VMEM((16, HD), i32),
                pltpu.VMEM((16, HD), i32),
                pltpu.VMEM((16, HD), i32),
                pltpu.VMEM((2,) + piece, bf16),
                pltpu.VMEM((3, 2) + piece, f32),
                pltpu.VMEM((2, 3) + piece, f32),
                pltpu.VMEM(piece, f32),
                pltpu.VMEM((ROUNDS, 2, 3) + piece, bf16),
                pltpu.VMEM((ROUNDS, 2, 3) + piece, bf16),
                pltpu.VMEM((ROUNDS,) + piece, f32),
                pltpu.VMEM((ROUNDS,) + piece, f32),
                pltpu.VMEM((ROUNDS, 3) + piece, f32),
                pltpu.VMEM((ROUNDS, 3) + piece, bf16),
                pltpu.VMEM((ROUNDS, 3) + piece, bf16),
                pltpu.VMEM((ROUNDS, 8, 256), f32),
                pltpu.VMEM((ROUNDS, 8, 256), f32),
                pltpu.VMEM((ROUNDS, 8, 256), f32),
                pltpu.VMEM((ROUNDS,) + piece, f32),
                pltpu.VMEM((ROUNDS, 2) + piece, bf16),
                pltpu.VMEM((ROUNDS, 2) + piece, bf16),
                pltpu.VMEM((ROUNDS, 8, 256), f32),
                pltpu.VMEM((ROUNDS, 2, 8, 256), f32),
                pltpu.SemaphoreType.DMA((5,)),
                pltpu.SemaphoreType.DMA((2,)),
                pltpu.SemaphoreType.DMA((2,)),
                pltpu.SemaphoreType.DMA((MESSAGES, ROUNDS)),
                pltpu.SemaphoreType.DMA((MESSAGES, ROUNDS)),
            ],
            compiler_params=pltpu.CompilerParams(
                collective_id=0, has_side_effects=True, vmem_limit_bytes=56 * 2**20
            ),
        )(order, tile_mask, reach, queries, keys, values, cache_keys, cache_values)

    placed = (
        P("tile", None, "slot"),
        P("tile", None, "slot"),
        P("tile", None, "slot"),
        P("slot", "tile", None, None),
        P("slot", "tile", None, None),
        P(),
        P("tile", None),
        P("tile", None),
    )
    return jax.shard_map(
        on_device, mesh=mesh, in_specs=placed, out_specs=P("tile", None, "slot"), check_vma=False
    )
```

```python
import functools
import math

import jax
import jax.numpy as jnp
from jax import lax
from jax.experimental import pallas as pl
from jax.experimental.pallas import tpu as pltpu
from jax.sharding import PartitionSpec as P

TH = 8
TW = 8
F = 3
HALO = 4
GX = 8
HD = 128
PAIRS = 22
TOKT = 192
STRETCHES = 4
HALF = 48
ROUNDS = 5
GROUPS = 4
NEGATIVE = -1e30
SCALE = math.log2(math.e) / math.sqrt(HD)
MESH = pl.DeviceIdType.MESH
U, O, D = 0, 1, 2
(
    Z_RIGHT0,
    Z_LEFT0,
    Z_RIGHT1,
    Z_LEFT1,
    Q_CHIP,
    Q_UP,
    Q_UP2,
    Q_DOWN,
    Q_PASS,
    Q_CORE0,
    Q_CORE2,
    P_CORE0,
    L_CORE0,
    P_CORE1,
    L_CORE1,
    P_CHIP0,
    L_CHIP0,
    P_CHIP1,
    L_CHIP1,
    P_UP,
    L_UP,
    P_DOWN,
    L_DOWN,
    MESSAGES,
) = range(24)


def nt_dot(a, b):
    return lax.dot_general(a, b, (((1,), (1,)), ((), ())), preferred_element_type=jnp.float32)


def dot(a, b):
    return lax.dot_general(a, b, (((1,), (0,)), ((), ())), preferred_element_type=jnp.float32)


def iota(shape, dim):
    return lax.broadcasted_iota(jnp.int32, shape, dim)


def spread(rows):
    padded = jnp.concatenate([rows, jnp.zeros((HD - rows.shape[0], 256), jnp.float32)], axis=0)
    return padded.T[:TOKT]


def gathered(columns):
    padded = jnp.concatenate([columns, jnp.zeros((256 - TOKT, HD), jnp.float32)], axis=0)
    return padded.T[:8]


def kernel(
    grid_rows,
    order_ref,
    mask_ref,
    reach_ref,
    q_hbm,
    k_hbm,
    v_hbm,
    ck_hbm,
    cv_hbm,
    out_ref,
    q_in,
    k_in,
    v_in,
    ck_in,
    cv_in,
    kv0,
    kv1,
    q,
    par,
    par_up,
    par_down,
    bias,
    table,
    part,
    lse,
    p1_send,
    p1_recv,
    l1_send,
    l1_recv,
    p2_send0,
    p2_recv0,
    p2_send1,
    p2_recv1,
    keep0,
    keep1,
    l2_rows,
    l2_recv,
    p3_send,
    p3_recv,
    l3_rows,
    l3_recv,
    in_sem,
    par_send_sem,
    par_recv_sem,
    send_sem,
    recv_sem,
):
    tile = lax.axis_index("tile")
    slot = lax.axis_index("slot")
    row, col = tile // GX, lax.rem(tile, GX)
    tiles = grid_rows * GX
    core_slot = slot + 1 - 2 * lax.rem(slot, 2)
    chip_slot = lax.rem(slot + 2, 4)
    right = row * GX + lax.rem(col + 1, GX)
    left = row * GX + lax.rem(col + GX - 1, GX)
    up = lax.rem(tile + tiles - GX, tiles)
    down = lax.rem(tile + GX, tiles)
    core_mate, chip_mate = (tile, core_slot), (tile, chip_slot)
    at_right, at_left = (right, slot), (left, slot)
    at_up, at_down = (up, chip_slot), (down, chip_slot)

    inputs = [
        pltpu.make_async_copy(source, target, in_sem.at[n])
        for n, (source, target) in enumerate(
            ((ck_hbm, ck_in), (cv_hbm, cv_in), (k_hbm, k_in), (v_hbm, v_in), (q_hbm, q_in))
        )
    ]
    for copy in inputs:
        copy.start()

    barrier = pltpu.get_barrier_semaphore()
    partners = (core_mate, chip_mate, at_right, at_left, at_up, at_down)
    for partner in partners:
        pl.semaphore_signal(barrier, inc=1, device_id=partner, device_id_type=MESH)

    def message(number, h, source, target, device):
        return pltpu.make_async_remote_copy(
            src_ref=source,
            dst_ref=target,
            send_sem=send_sem.at[number, h],
            recv_sem=recv_sem.at[number, h],
            device_id=device,
            device_id_type=MESH,
        )

    messages = {
        Z_RIGHT0: lambda h: message(Z_RIGHT0, h, kv0.at[h, 2], kv0.at[h, 0], at_right),
        Z_LEFT0: lambda h: message(Z_LEFT0, h, kv0.at[h, 1], kv0.at[h, 3], at_left),
        Z_RIGHT1: lambda h: message(Z_RIGHT1, h, kv1.at[h, 2], kv1.at[h, 0], at_right),
        Z_LEFT1: lambda h: message(Z_LEFT1, h, kv1.at[h, 1], kv1.at[h, 3], at_left),
        Q_CHIP: lambda h: message(Q_CHIP, h, q.at[h, 0, O], q.at[h, 2, O], chip_mate),
        Q_UP: lambda h: message(Q_UP, h, q.at[h, 0, O], q.at[h, 2, D], at_up),
        Q_UP2: lambda h: message(Q_UP2, h, q.at[h, 2, O], q.at[h, 0, D], at_up),
        Q_DOWN: lambda h: message(Q_DOWN, h, q.at[h, 0, O], q.at[h, 2, U], at_down),
        Q_PASS: lambda h: message(Q_PASS, h, q.at[h, 2, U], q.at[h, 0, U], chip_mate),
        Q_CORE0: lambda h: message(Q_CORE0, h, q.at[h, 0], q.at[h, 1], core_mate),
        Q_CORE2: lambda h: message(Q_CORE2, h, q.at[h, 2], q.at[h, 3], core_mate),
        P_CORE0: lambda h: message(P_CORE0, h, p1_send.at[h, 0], p1_recv.at[h, 0], core_mate),
        L_CORE0: lambda h: message(L_CORE0, h, l1_send.at[h, 0], l1_recv.at[h, 0], core_mate),
        P_CORE1: lambda h: message(P_CORE1, h, p1_send.at[h, 1], p1_recv.at[h, 1], core_mate),
        L_CORE1: lambda h: message(L_CORE1, h, l1_send.at[h, 1], l1_recv.at[h, 1], core_mate),
        P_CHIP0: lambda h: message(P_CHIP0, h, p2_send0.at[h], p2_recv0.at[h], chip_mate),
        L_CHIP0: lambda h: message(L_CHIP0, h, l2_rows.at[h, 0], l2_recv.at[h, 0], chip_mate),
        P_CHIP1: lambda h: message(P_CHIP1, h, p2_send1.at[h], p2_recv1.at[h], chip_mate),
        L_CHIP1: lambda h: message(L_CHIP1, h, l2_rows.at[h, 1], l2_recv.at[h, 1], chip_mate),
        P_UP: lambda h: message(P_UP, h, p3_send.at[h, 0], p3_recv.at[h, 0], at_up),
        L_UP: lambda h: message(L_UP, h, l3_rows.at[h], l3_recv.at[h, 0], at_up),
        P_DOWN: lambda h: message(P_DOWN, h, p3_send.at[h, 1], p3_recv.at[h, 1], at_down),
        L_DOWN: lambda h: message(L_DOWN, h, l3_rows.at[h], l3_recv.at[h, 1], at_down),
    }

    def start(h, *numbers):
        for number in numbers:
            messages[number](h).start()

    def arrived(h, *numbers):
        for number in numbers:
            messages[number](h).wait_recv()

    age = jnp.int32(0)
    for n in range(STRETCHES):
        age = age + jnp.where(slot == n, order_ref[n], 0)
    sub, lane = iota((8, HD), 0), iota((8, HD), 1)
    moment = jnp.where(sub < F, (STRETCHES - 1 - age) * F + sub, STRETCHES * F + sub - F)
    pair = jnp.where(lane < PAIRS, lane, lane - PAIRS).astype(jnp.float32)
    frequency = jnp.exp(pair * (-math.log(10000.0) / PAIRS))
    angle = jnp.where(lane < 2 * PAIRS, moment.astype(jnp.float32) * frequency, 0.0)
    cosine, sine = jnp.cos(angle), jnp.sin(angle)
    for n in range(2):
        for f in range(F):
            for at, values in ((0, cosine), (1, sine)):
                wanted = jnp.broadcast_to(values[n * F + f : n * F + f + 1], (16, HD))
                for quarter in range(4):
                    table[n, at, pl.ds(quarter * HALF + f * 16, 16)] = wanted
                if n == 1:
                    for part_at in range(4):
                        table[2, at, pl.ds(f * 64 + part_at * 16, 16)] = wanted

    first, second = iota((HD, HD), 0), iota((HD, HD), 1)
    exchange = jnp.where(
        (second < PAIRS) & (first == second + PAIRS),
        -1.0,
        jnp.where((second >= PAIRS) & (second < 2 * PAIRS) & (first == second - PAIRS), 1.0, 0.0),
    ).astype(jnp.bfloat16)
    at = iota((TOKT, TOKT), 0)
    side = (at >= 2 * HALF).astype(jnp.int32)
    rest = at - side * 2 * HALF
    lower = (rest >= HALF).astype(jnp.int32)
    rest = rest - lower * HALF
    source = (
        (rest >> 4) * TH * TW + (lower * HALO + ((rest >> 2) & 3)) * TW + side * HALO + (rest & 3)
    )
    quarters = (iota((TOKT, TOKT), 1) == source).astype(jnp.float32).astype(jnp.bfloat16)

    def turned(x, n):
        swapped = dot(x.astype(jnp.bfloat16), exchange)
        return x.astype(jnp.float32) * table[n, 0] + swapped * table[n, 1]

    def group_of(e):
        if e == 0:
            return slot
        if e == 1:
            return core_slot
        if e == 2:
            return chip_slot
        return 3 - slot

    def prepare_block(h, kv, e, keys, values, n):
        both = dot(quarters, jnp.concatenate([keys, values], axis=1))
        new_keys = turned(both[:, :HD], n).astype(jnp.bfloat16)
        new_values = both[:, HD:].astype(jnp.bfloat16)
        for g in range(2):
            for lower_half in range(2):
                at_row = (g * 2 + lower_half) * HALF
                kv[h, 1 + g, 0, e, lower_half] = new_keys[at_row : at_row + HALF]
                kv[h, 1 + g, 1, e, lower_half] = new_values[at_row : at_row + HALF]

    def prepare(h):
        for e in range(GROUPS):
            lanes = pl.ds(pl.multiple_of((group_of(e) * ROUNDS + h) * HD, HD), HD)
            kv = kv0 if e < 2 else kv1
            prepare_block(h, kv, e % 2, ck_in[0, 0, :, lanes], cv_in[0, 0, :, lanes], 0)
        lanes = pl.ds(pl.multiple_of(h * HD, HD), HD)
        prepare_block(h, kv0, 2, k_in[0, :, lanes], v_in[0, :, lanes], 1)
        q[h, 0, O] = turned(q_in[0, :, lanes], 2).astype(jnp.bfloat16)

    entry = iota((16, HD), 0)
    block = jnp.zeros((16, HD), jnp.int32)
    for n in range(9):
        block = jnp.where(entry == n, mask_ref[0, n], block)
    for n in range(2):
        block = jnp.where(entry == 9 + n, reach_ref[0, n], block)
    par[...] = block

    for copy in inputs:
        copy.wait()
    prepare(0)
    pl.semaphore_wait(barrier, len(partners))

    par_copies = [
        pltpu.make_async_remote_copy(
            src_ref=par,
            dst_ref=target,
            send_sem=par_send_sem.at[n],
            recv_sem=par_recv_sem.at[n],
            device_id=device,
            device_id_type=MESH,
        )
        for n, (target, device) in enumerate(((par_up, at_down), (par_down, at_up)))
    ]
    for copy in par_copies:
        copy.start()

    def relay(h):
        arrived(h, Q_CHIP)
        start(h, Q_UP2)
        arrived(h, Q_DOWN)
        start(h, Q_PASS)

    def share(h):
        arrived(h, Q_UP)
        start(h, Q_CORE2)
        arrived(h, Q_PASS, Q_UP2)
        start(h, Q_CORE0)

    def ask(h):
        start(h, Q_CHIP, Q_DOWN, Q_UP)

    start(0, Z_RIGHT0, Z_LEFT0, Z_RIGHT1, Z_LEFT1)
    ask(0)

    def first_sends(h, carry):
        prepare(h)
        start(h, Z_RIGHT0, Z_LEFT0, Z_RIGHT1, Z_LEFT1)

        @pl.when(h == 1)
        def _():
            ask(1)

        return carry

    lax.fori_loop(1, ROUNDS, first_sends, 0)
    relay(0)
    ask(2)

    for copy in par_copies:
        copy.wait_recv()

    key, feature = iota((TOKT, HD), 0), iota((TOKT, HD), 1)
    from_left, from_right = key < HALF, key >= 3 * HALF
    key_row, key_col = (key >> 2) & 3, key & 3

    def window(values, dy, rows_good):
        bits = [values[(dy + 1) * 3 + n : (dy + 1) * 3 + n + 1] for n in range(3)]
        reach_cols = values[10:11]
        middle = jnp.full((1, HD), 1, jnp.int32) if dy == 0 else bits[1]
        on_left = from_left & (key_col >= HALO - reach_cols) & (bits[0] > 0) & (col >= 1)
        on_right = from_right & (key_col < reach_cols) & (bits[2] > 0) & (col < GX - 1)
        inside = (key >= HALF) & (key < 3 * HALF) & (middle > 0)
        good = (on_left | on_right | inside) & rows_good
        return jnp.where(good, 0.0, NEGATIVE)

    above, below, here = par_up[...], par_down[...], par[...]
    own_window = window(here, 0, key >= 0)
    up_window = window(above, 1, (key_row < above[9:10]) & (row >= 1))
    down_window = window(below, -1, (key_row >= HALO - below[9:10]) & (row < grid_rows - 1))
    for n, other in enumerate((up_window, down_window)):
        bias[n] = jnp.where(
            feature == 0, other, jnp.where(feature == 1, own_window, 0.0)
        ).astype(jnp.bfloat16)

    def compute(h, groups):
        other_marker = jnp.where(feature == 0, 1.0, 0.0).astype(jnp.bfloat16)
        own_marker = jnp.where(feature == 1, 1.0, 0.0).astype(jnp.bfloat16)
        ones = jnp.ones((TOKT, HD), jnp.bfloat16)
        markers = (
            jnp.concatenate([other_marker, own_marker], axis=0),
            jnp.concatenate([own_marker, other_marker], axis=0),
        )
        all_levels = []
        for e in groups:
            levels = jnp.zeros((TOKT, HD), jnp.float32)
            kv = kv0 if e < 2 else kv1
            blocks = (e % 2,) if e > 0 else (0, 2)
            scores, highest = [], []
            for half in range(2):
                keys = jnp.concatenate(
                    [
                        jnp.concatenate(
                            [kv[h, :, 0, n, half].reshape(TOKT, HD), bias[half]], axis=1
                        )
                        for n in blocks
                    ],
                    axis=0,
                )
                queries = q[h, e, pl.ds(half, 2)].reshape(2 * TOKT, HD)
                found = nt_dot(jnp.concatenate([queries, markers[half]], axis=1), keys)
                scores.append(found)
                highest.append(jnp.max(found, axis=1, keepdims=True))
            top, bottom = highest
            own = jnp.maximum(top[TOKT:], bottom[:TOKT])
            highest = (
                jnp.concatenate([top[:TOKT], own], axis=0),
                jnp.concatenate([own, bottom[TOKT:]], axis=0),
            )
            summed = []
            for half in range(2):
                weights = jnp.exp2((scores[half] - highest[half]) * SCALE).astype(jnp.bfloat16)
                values = jnp.concatenate(
                    [
                        jnp.concatenate([kv[h, :, 1, n, half].reshape(TOKT, HD), ones], axis=1)
                        for n in blocks
                    ],
                    axis=0,
                )
                summed.append(dot(weights, values))
            for tile_kind, result, level in (
                (U, summed[0][:TOKT], top[:TOKT]),
                (O, summed[0][TOKT:] + summed[1][:TOKT], own),
                (D, summed[1][TOKT:], bottom[TOKT:]),
            ):
                total = result[:, HD:]
                level = level * SCALE + jnp.log2(total)
                result = result[:, :HD] / total
                if e % 2 == 0:
                    part[e // 2, tile_kind] = result
                else:
                    p1_send[h, e // 2, tile_kind] = result.astype(jnp.bfloat16)
                levels = jnp.where(feature == tile_kind, level, levels)
            all_levels.append(levels)
        return all_levels

    def after_core(h, n):
        arrived(h, *((P_CORE0, L_CORE0) if n == 0 else (P_CORE1, L_CORE1)))
        mine, theirs = lse[n], l1_recv[h, n]
        newest = jnp.maximum(mine, theirs)
        mine_part, theirs_part = jnp.exp2(mine - newest), jnp.exp2(theirs - newest)
        total = mine_part + theirs_part
        mine_part, theirs_part = mine_part / total, theirs_part / total
        for tile_kind in range(3):
            result = (
                part[n, tile_kind] * mine_part[:, tile_kind : tile_kind + 1]
                + p1_recv[h, n, tile_kind].astype(jnp.float32)
                * theirs_part[:, tile_kind : tile_kind + 1]
            )
            if n == 0:
                if tile_kind == O:
                    keep0[h] = result
                else:
                    p2_send0[h, tile_kind // 2] = result.astype(jnp.bfloat16)
            elif tile_kind == O:
                p2_send1[h] = result.astype(jnp.bfloat16)
            else:
                keep1[h, tile_kind // 2] = result
        start(h, P_CHIP0 if n == 0 else P_CHIP1)
        l2_rows[h, n] = gathered(newest + jnp.log2(total))
        start(h, L_CHIP0 if n == 0 else L_CHIP1)

    def after_chip(h):
        arrived(h, P_CHIP0, L_CHIP0)
        mine, theirs = l2_rows[h, 1], l2_recv[h, 0]
        newest = jnp.maximum(mine, theirs)
        mine_part, theirs_part = jnp.exp2(mine - newest), jnp.exp2(theirs - newest)
        total = mine_part + theirs_part
        l3_rows[h] = newest + jnp.log2(total)
        start(h, L_UP, L_DOWN)
        columns = spread(jnp.concatenate([mine_part / total, theirs_part / total], axis=0))
        for n, (tile_kind, number) in enumerate(((U, P_UP), (D, P_DOWN))):
            result = (
                keep1[h, n] * columns[:, tile_kind : tile_kind + 1]
                + p2_recv0[h, n].astype(jnp.float32) * columns[:, 8 + tile_kind : 9 + tile_kind]
            )
            p3_send[h, n] = result.astype(jnp.bfloat16)
            start(h, number)

    def after_row(h):
        arrived(h, P_CHIP1, L_CHIP1, P_UP, L_UP, P_DOWN, L_DOWN)
        levels = (
            l2_rows[h, 0][O : O + 1],
            l2_recv[h, 1][O : O + 1],
            l3_recv[h, 0][U : U + 1],
            l3_recv[h, 1][D : D + 1],
        )
        newest = functools.reduce(jnp.maximum, levels)
        parts = [jnp.exp2(x - newest) for x in levels]
        total = parts[0] + parts[1] + parts[2] + parts[3]
        columns = spread(
            jnp.concatenate(
                [x / total for x in parts] + [jnp.zeros((4, 256), jnp.float32)], axis=0
            )
        )
        result = (
            keep0[h] * columns[:, 0:1]
            + p2_recv1[h].astype(jnp.float32) * columns[:, 1:2]
            + p3_recv[h, 0].astype(jnp.float32) * columns[:, 2:3]
            + p3_recv[h, 1].astype(jnp.float32) * columns[:, 3:4]
        )
        lanes = pl.ds(pl.multiple_of(h * HD, HD), HD)
        out_ref[0, :, lanes] = result.astype(jnp.bfloat16)

    share(0)
    relay(1)
    ask(3)

    def step(i, carry):
        arrived(i, Q_CORE0, Q_CORE2, Z_RIGHT0, Z_LEFT0, Z_RIGHT1, Z_LEFT1)
        l1_send[i, 0], l1_send[i, 1], lse[0], lse[1] = compute(i, (1, 3, 0, 2))
        start(i, P_CORE0, L_CORE0, P_CORE1, L_CORE1)
        share(i + 1)

        @pl.when(i + 2 < ROUNDS)
        def _():
            relay(i + 2)

        @pl.when(i + 4 < ROUNDS)
        def _():
            ask(i + 4)

        after_core(i, 0)
        after_core(i, 1)

        @pl.when(i >= 1)
        def _():
            after_chip(i - 1)

        @pl.when(i >= 2)
        def _():
            after_row(i - 2)

        return carry

    lax.fori_loop(0, ROUNDS - 1, step, 0)

    last = ROUNDS - 1
    arrived(last, Q_CORE0, Q_CORE2, Z_RIGHT0, Z_LEFT0)
    l1_send[last, 0], lse[0] = compute(last, (1, 0))
    start(last, P_CORE0, L_CORE0)
    after_core(last, 0)
    arrived(last, Z_RIGHT1, Z_LEFT1)
    l1_send[last, 1], lse[1] = compute(last, (3, 2))
    start(last, P_CORE1, L_CORE1)
    after_chip(last - 1)
    after_core(last, 1)
    after_chip(last)
    after_row(last - 2)
    after_row(last - 1)
    after_row(last)

    def finish(h, carry):
        for number in range(MESSAGES):
            messages[number](h).wait_send()
        return carry

    lax.fori_loop(0, ROUNDS, finish, 0)
    for copy in par_copies:
        copy.wait_send()


def solution(mesh):
    grid_rows = mesh.shape["tile"] // GX
    bf16, f32, i32 = jnp.bfloat16, jnp.float32, jnp.int32
    wide = GROUPS * ROUNDS * HD

    def on_device(queries, keys, values, cache_keys, cache_values, order, tile_mask, reach):
        smem = pl.BlockSpec(memory_space=pltpu.SMEM)
        anywhere = pl.BlockSpec(memory_space=pl.ANY)
        piece = (TOKT, HD)
        return pl.pallas_call(
            functools.partial(kernel, grid_rows),
            out_shape=jax.ShapeDtypeStruct((1, TOKT, ROUNDS * HD), bf16),
            in_specs=[smem] * 3 + [anywhere] * 5,
            out_specs=pl.BlockSpec(memory_space=pltpu.VMEM),
            scratch_shapes=[
                pltpu.VMEM((1, TOKT, ROUNDS * HD), bf16),
                pltpu.VMEM((1, TOKT, ROUNDS * HD), bf16),
                pltpu.VMEM((1, TOKT, ROUNDS * HD), bf16),
                pltpu.VMEM((1, 1, TOKT, wide), bf16),
                pltpu.VMEM((1, 1, TOKT, wide), bf16),
                pltpu.VMEM((ROUNDS, 4, 2, 3, 2, HALF, HD), bf16),
                pltpu.VMEM((ROUNDS, 4, 2, 2, 2, HALF, HD), bf16),
                pltpu.VMEM((ROUNDS, GROUPS, 3) + piece, bf16),
                pltpu.VMEM((16, HD), i32),
                pltpu.VMEM((16, HD), i32),
                pltpu.VMEM((16, HD), i32),
                pltpu.VMEM((2,) + piece, bf16),
                pltpu.VMEM((3, 2) + piece, f32),
                pltpu.VMEM((2, 3) + piece, f32),
                pltpu.VMEM((2,) + piece, f32),
                pltpu.VMEM((ROUNDS, 2, 3) + piece, bf16),
                pltpu.VMEM((ROUNDS, 2, 3) + piece, bf16),
                pltpu.VMEM((ROUNDS, 2) + piece, f32),
                pltpu.VMEM((ROUNDS, 2) + piece, f32),
                pltpu.VMEM((ROUNDS, 2) + piece, bf16),
                pltpu.VMEM((ROUNDS, 2) + piece, bf16),
                pltpu.VMEM((ROUNDS,) + piece, bf16),
                pltpu.VMEM((ROUNDS,) + piece, bf16),
                pltpu.VMEM((ROUNDS,) + piece, f32),
                pltpu.VMEM((ROUNDS, 2) + piece, f32),
                pltpu.VMEM((ROUNDS, 2, 8, 256), f32),
                pltpu.VMEM((ROUNDS, 2, 8, 256), f32),
                pltpu.VMEM((ROUNDS, 2) + piece, bf16),
                pltpu.VMEM((ROUNDS, 2) + piece, bf16),
                pltpu.VMEM((ROUNDS, 8, 256), f32),
                pltpu.VMEM((ROUNDS, 2, 8, 256), f32),
                pltpu.SemaphoreType.DMA((5,)),
                pltpu.SemaphoreType.DMA((2,)),
                pltpu.SemaphoreType.DMA((2,)),
                pltpu.SemaphoreType.DMA((MESSAGES, ROUNDS)),
                pltpu.SemaphoreType.DMA((MESSAGES, ROUNDS)),
            ],
            compiler_params=pltpu.CompilerParams(
                collective_id=0, has_side_effects=True, vmem_limit_bytes=56 * 2**20
            ),
        )(order, tile_mask, reach, queries, keys, values, cache_keys, cache_values)

    placed = (
        P("tile", None, "slot"),
        P("tile", None, "slot"),
        P("tile", None, "slot"),
        P("slot", "tile", None, None),
        P("slot", "tile", None, None),
        P(),
        P("tile", None),
        P("tile", None),
    )
    return jax.shard_map(
        on_device, mesh=mesh, in_specs=placed, out_specs=P("tile", None, "slot"), check_vma=False
    )
```

```python
import functools
import math

import jax
import jax.numpy as jnp
from jax import lax
from jax.experimental import pallas as pl
from jax.experimental.pallas import tpu as pltpu
from jax.sharding import PartitionSpec as P

TH = 8
TW = 8
F = 3
HALO = 4
GX = 8
HD = 128
PAIRS = 22
TOKT = 192
STRETCHES = 4
HALF = 48
ROUNDS = 5
GROUPS = 4
NEGATIVE = -1e30
SCALE = math.log2(math.e) / math.sqrt(HD)
MESH = pl.DeviceIdType.MESH
U, O, D = 0, 1, 2
(
    Z_RIGHT0,
    Z_LEFT0,
    Z_RIGHT1,
    Z_LEFT1,
    Q_CHIP,
    Q_UP,
    Q_UP2,
    Q_DOWN,
    Q_PASS,
    Q_CORE0,
    Q_CORE2,
    P_CORE0,
    L_CORE0,
    P_CORE1,
    L_CORE1,
    P_CHIP0,
    L_CHIP0,
    P_CHIP1,
    L_CHIP1,
    P_UP,
    L_UP,
    P_DOWN,
    L_DOWN,
    MESSAGES,
) = range(24)


def nt_dot(a, b):
    return lax.dot_general(a, b, (((1,), (1,)), ((), ())), preferred_element_type=jnp.float32)


def dot(a, b):
    return lax.dot_general(a, b, (((1,), (0,)), ((), ())), preferred_element_type=jnp.float32)


def iota(shape, dim):
    return lax.broadcasted_iota(jnp.int32, shape, dim)


def spread(rows):
    padded = jnp.concatenate([rows, jnp.zeros((HD - rows.shape[0], 256), jnp.float32)], axis=0)
    return padded.T[:TOKT]


def gathered(columns):
    padded = jnp.concatenate([columns, jnp.zeros((256 - TOKT, HD), jnp.float32)], axis=0)
    return padded.T[:8]


def kernel(
    grid_rows,
    order_ref,
    mask_ref,
    reach_ref,
    q_hbm,
    k_hbm,
    v_hbm,
    ck_hbm,
    cv_hbm,
    out_ref,
    q_in,
    k_in,
    v_in,
    ck_in,
    cv_in,
    kv0,
    kv1,
    q,
    par,
    par_up,
    par_down,
    bias,
    table,
    part,
    lse,
    p1_send,
    p1_recv,
    l1_send,
    l1_recv,
    p2_send0,
    p2_recv0,
    p2_send1,
    p2_recv1,
    keep0,
    keep1,
    l2_rows,
    l2_recv,
    p3_send,
    p3_recv,
    l3_rows,
    l3_recv,
    in_sem,
    par_send_sem,
    par_recv_sem,
    send_sem,
    recv_sem,
):
    tile = lax.axis_index("tile")
    slot = lax.axis_index("slot")
    row, col = tile // GX, lax.rem(tile, GX)
    tiles = grid_rows * GX
    core_slot = slot + 1 - 2 * lax.rem(slot, 2)
    chip_slot = lax.rem(slot + 2, 4)
    right = row * GX + lax.rem(col + 1, GX)
    left = row * GX + lax.rem(col + GX - 1, GX)
    up = lax.rem(tile + tiles - GX, tiles)
    down = lax.rem(tile + GX, tiles)
    core_mate, chip_mate = (tile, core_slot), (tile, chip_slot)
    at_right, at_left = (right, slot), (left, slot)
    at_up, at_down = (up, chip_slot), (down, chip_slot)

    inputs = [
        pltpu.make_async_copy(source, target, in_sem.at[n])
        for n, (source, target) in enumerate(
            ((ck_hbm, ck_in), (cv_hbm, cv_in), (k_hbm, k_in), (v_hbm, v_in), (q_hbm, q_in))
        )
    ]
    for copy in inputs:
        copy.start()

    barrier = pltpu.get_barrier_semaphore()
    partners = (core_mate, chip_mate, at_right, at_left, at_up, at_down)
    for partner in partners:
        pl.semaphore_signal(barrier, inc=1, device_id=partner, device_id_type=MESH)

    def message(number, h, source, target, device):
        return pltpu.make_async_remote_copy(
            src_ref=source,
            dst_ref=target,
            send_sem=send_sem.at[number, h],
            recv_sem=recv_sem.at[number, h],
            device_id=device,
            device_id_type=MESH,
        )

    messages = {
        Z_RIGHT0: lambda h: message(Z_RIGHT0, h, kv0.at[h, 2], kv0.at[h, 0], at_right),
        Z_LEFT0: lambda h: message(Z_LEFT0, h, kv0.at[h, 1], kv0.at[h, 3], at_left),
        Z_RIGHT1: lambda h: message(Z_RIGHT1, h, kv1.at[h, 2], kv1.at[h, 0], at_right),
        Z_LEFT1: lambda h: message(Z_LEFT1, h, kv1.at[h, 1], kv1.at[h, 3], at_left),
        Q_CHIP: lambda h: message(Q_CHIP, h, q.at[h, 0, O], q.at[h, 2, O], chip_mate),
        Q_UP: lambda h: message(Q_UP, h, q.at[h, 0, O], q.at[h, 2, D], at_up),
        Q_UP2: lambda h: message(Q_UP2, h, q.at[h, 2, O], q.at[h, 0, D], at_up),
        Q_DOWN: lambda h: message(Q_DOWN, h, q.at[h, 0, O], q.at[h, 2, U], at_down),
        Q_PASS: lambda h: message(Q_PASS, h, q.at[h, 2, U], q.at[h, 0, U], chip_mate),
        Q_CORE0: lambda h: message(Q_CORE0, h, q.at[h, 0], q.at[h, 1], core_mate),
        Q_CORE2: lambda h: message(Q_CORE2, h, q.at[h, 2], q.at[h, 3], core_mate),
        P_CORE0: lambda h: message(P_CORE0, h, p1_send.at[h, 0], p1_recv.at[h, 0], core_mate),
        L_CORE0: lambda h: message(L_CORE0, h, l1_send.at[h, 0], l1_recv.at[h, 0], core_mate),
        P_CORE1: lambda h: message(P_CORE1, h, p1_send.at[h, 1], p1_recv.at[h, 1], core_mate),
        L_CORE1: lambda h: message(L_CORE1, h, l1_send.at[h, 1], l1_recv.at[h, 1], core_mate),
        P_CHIP0: lambda h: message(P_CHIP0, h, p2_send0.at[h], p2_recv0.at[h], chip_mate),
        L_CHIP0: lambda h: message(L_CHIP0, h, l2_rows.at[h, 0], l2_recv.at[h, 0], chip_mate),
        P_CHIP1: lambda h: message(P_CHIP1, h, p2_send1.at[h], p2_recv1.at[h], chip_mate),
        L_CHIP1: lambda h: message(L_CHIP1, h, l2_rows.at[h, 1], l2_recv.at[h, 1], chip_mate),
        P_UP: lambda h: message(P_UP, h, p3_send.at[h, 0], p3_recv.at[h, 0], at_up),
        L_UP: lambda h: message(L_UP, h, l3_rows.at[h], l3_recv.at[h, 0], at_up),
        P_DOWN: lambda h: message(P_DOWN, h, p3_send.at[h, 1], p3_recv.at[h, 1], at_down),
        L_DOWN: lambda h: message(L_DOWN, h, l3_rows.at[h], l3_recv.at[h, 1], at_down),
    }

    def start(h, *numbers):
        for number in numbers:
            messages[number](h).start()

    def arrived(h, *numbers):
        for number in numbers:
            messages[number](h).wait_recv()

    age = jnp.int32(0)
    for n in range(STRETCHES):
        age = age + jnp.where(slot == n, order_ref[n], 0)
    sub, lane = iota((8, HD), 0), iota((8, HD), 1)
    moment = jnp.where(sub < F, (STRETCHES - 1 - age) * F + sub, STRETCHES * F + sub - F)
    pair = jnp.where(lane < PAIRS, lane, lane - PAIRS).astype(jnp.float32)
    frequency = jnp.exp(pair * (-math.log(10000.0) / PAIRS))
    angle = jnp.where(lane < 2 * PAIRS, moment.astype(jnp.float32) * frequency, 0.0)
    cosine, sine = jnp.cos(angle), jnp.sin(angle)
    for n in range(2):
        for f in range(F):
            for at, values in ((0, cosine), (1, sine)):
                wanted = jnp.broadcast_to(values[n * F + f : n * F + f + 1], (16, HD))
                for quarter in range(4):
                    table[n, at, pl.ds(quarter * HALF + f * 16, 16)] = wanted
                if n == 1:
                    for part_at in range(4):
                        table[2, at, pl.ds(f * 64 + part_at * 16, 16)] = wanted

    first, second = iota((HD, HD), 0), iota((HD, HD), 1)
    exchange = jnp.where(
        (second < PAIRS) & (first == second + PAIRS),
        -1.0,
        jnp.where((second >= PAIRS) & (second < 2 * PAIRS) & (first == second - PAIRS), 1.0, 0.0),
    ).astype(jnp.bfloat16)
    at = iota((TOKT, TOKT), 0)
    side = (at >= 2 * HALF).astype(jnp.int32)
    rest = at - side * 2 * HALF
    lower = (rest >= HALF).astype(jnp.int32)
    rest = rest - lower * HALF
    source = (
        (rest >> 4) * TH * TW + (lower * HALO + ((rest >> 2) & 3)) * TW + side * HALO + (rest & 3)
    )
    quarters = (iota((TOKT, TOKT), 1) == source).astype(jnp.float32).astype(jnp.bfloat16)

    def turned(x, n):
        swapped = dot(x.astype(jnp.bfloat16), exchange)
        return x.astype(jnp.float32) * table[n, 0] + swapped * table[n, 1]

    def group_of(e):
        if e == 0:
            return slot
        if e == 1:
            return core_slot
        if e == 2:
            return chip_slot
        return 3 - slot

    def prepare_block(h, kv, e, keys, values, n):
        both = dot(quarters, jnp.concatenate([keys, values], axis=1))
        new_keys = turned(both[:, :HD], n).astype(jnp.bfloat16)
        new_values = both[:, HD:].astype(jnp.bfloat16)
        for g in range(2):
            for lower_half in range(2):
                at_row = (g * 2 + lower_half) * HALF
                kv[h, 1 + g, 0, e, lower_half] = new_keys[at_row : at_row + HALF]
                kv[h, 1 + g, 1, e, lower_half] = new_values[at_row : at_row + HALF]

    def prepare(h):
        for e in range(GROUPS):
            lanes = pl.ds(pl.multiple_of((group_of(e) * ROUNDS + h) * HD, HD), HD)
            kv = kv0 if e < 2 else kv1
            prepare_block(h, kv, e % 2, ck_in[0, 0, :, lanes], cv_in[0, 0, :, lanes], 0)
        lanes = pl.ds(pl.multiple_of(h * HD, HD), HD)
        prepare_block(h, kv0, 2, k_in[0, :, lanes], v_in[0, :, lanes], 1)
        q[h, 0, O] = turned(q_in[0, :, lanes], 2).astype(jnp.bfloat16)

    entry = iota((16, HD), 0)
    block = jnp.zeros((16, HD), jnp.int32)
    for n in range(9):
        block = jnp.where(entry == n, mask_ref[0, n], block)
    for n in range(2):
        block = jnp.where(entry == 9 + n, reach_ref[0, n], block)
    par[...] = block

    for copy in inputs:
        copy.wait()
    prepare(0)
    pl.semaphore_wait(barrier, len(partners))

    par_copies = [
        pltpu.make_async_remote_copy(
            src_ref=par,
            dst_ref=target,
            send_sem=par_send_sem.at[n],
            recv_sem=par_recv_sem.at[n],
            device_id=device,
            device_id_type=MESH,
        )
        for n, (target, device) in enumerate(((par_up, at_down), (par_down, at_up)))
    ]
    for copy in par_copies:
        copy.start()

    def relay(h):
        arrived(h, Q_CHIP)
        start(h, Q_UP2)
        arrived(h, Q_DOWN)
        start(h, Q_PASS)

    def share(h):
        arrived(h, Q_UP)
        start(h, Q_CORE2)
        arrived(h, Q_PASS, Q_UP2)
        start(h, Q_CORE0)

    def ask(h):
        start(h, Q_CHIP, Q_DOWN, Q_UP)

    start(0, Z_RIGHT0, Z_LEFT0, Z_RIGHT1, Z_LEFT1)
    ask(0)

    def first_sends(h, carry):
        prepare(h)
        start(h, Z_RIGHT0, Z_LEFT0, Z_RIGHT1, Z_LEFT1)

        @pl.when(h == 1)
        def _():
            ask(1)

        return carry

    lax.fori_loop(1, ROUNDS, first_sends, 0)
    relay(0)
    ask(2)

    for copy in par_copies:
        copy.wait_recv()

    key, feature = iota((TOKT, HD), 0), iota((TOKT, HD), 1)
    from_left, from_right = key < HALF, key >= 3 * HALF
    key_row, key_col = (key >> 2) & 3, key & 3

    def window(values, dy, rows_good):
        bits = [values[(dy + 1) * 3 + n : (dy + 1) * 3 + n + 1] for n in range(3)]
        reach_cols = values[10:11]
        middle = jnp.full((1, HD), 1, jnp.int32) if dy == 0 else bits[1]
        on_left = from_left & (key_col >= HALO - reach_cols) & (bits[0] > 0) & (col >= 1)
        on_right = from_right & (key_col < reach_cols) & (bits[2] > 0) & (col < GX - 1)
        inside = (key >= HALF) & (key < 3 * HALF) & (middle > 0)
        good = (on_left | on_right | inside) & rows_good
        return jnp.where(good, 0.0, NEGATIVE)

    above, below, here = par_up[...], par_down[...], par[...]
    own_window = window(here, 0, key >= 0)
    up_window = window(above, 1, (key_row < above[9:10]) & (row >= 1))
    down_window = window(below, -1, (key_row >= HALO - below[9:10]) & (row < grid_rows - 1))
    for n, other in enumerate((up_window, down_window)):
        bias[n] = jnp.where(
            feature == 0, other, jnp.where(feature == 1, own_window, 0.0)
        ).astype(jnp.bfloat16)

    def compute(h, groups):
        other_marker = jnp.where(feature == 0, 1.0, 0.0).astype(jnp.bfloat16)
        own_marker = jnp.where(feature == 1, 1.0, 0.0).astype(jnp.bfloat16)
        ones = jnp.ones((TOKT, HD), jnp.bfloat16)
        nothing = jnp.concatenate(
            [jnp.zeros((64, HD), jnp.bfloat16), jnp.full((64, HD), NEGATIVE, jnp.bfloat16)], axis=1
        )
        markers = (
            jnp.concatenate([other_marker, own_marker], axis=0),
            jnp.concatenate([own_marker, other_marker], axis=0),
        )
        all_levels = []
        for e in groups:
            levels = jnp.zeros((TOKT, HD), jnp.float32)
            kv = kv0 if e < 2 else kv1
            blocks = (e % 2,) if e > 0 else (0, 2)
            scores, highest = [], []
            for half in range(2):
                keys = jnp.concatenate(
                    [
                        jnp.concatenate(
                            [kv[h, :, 0, n, half].reshape(TOKT, HD), bias[half]], axis=1
                        )
                        for n in blocks
                    ]
                    + ([nothing] if len(blocks) == 1 else []),
                    axis=0,
                )
                queries = q[h, e, pl.ds(half, 2)].reshape(2 * TOKT, HD)
                found = nt_dot(jnp.concatenate([queries, markers[half]], axis=1), keys)
                scores.append(found)
                highest.append(jnp.max(found, axis=1, keepdims=True))
            top, bottom = highest
            own = jnp.maximum(top[TOKT:], bottom[:TOKT])
            highest = (
                jnp.concatenate([top[:TOKT], own], axis=0),
                jnp.concatenate([own, bottom[TOKT:]], axis=0),
            )
            summed = []
            for half in range(2):
                weights = jnp.exp2(scores[half] * SCALE - highest[half] * SCALE).astype(jnp.bfloat16)
                values = jnp.concatenate(
                    [
                        jnp.concatenate([kv[h, :, 1, n, half].reshape(TOKT, HD), ones], axis=1)
                        for n in blocks
                    ]
                    + ([jnp.zeros((64, 2 * HD), jnp.bfloat16)] if len(blocks) == 1 else []),
                    axis=0,
                )
                summed.append(dot(weights, values))
            for tile_kind, result, level in (
                (U, summed[0][:TOKT], top[:TOKT]),
                (O, summed[0][TOKT:] + summed[1][:TOKT], own),
                (D, summed[1][TOKT:], bottom[TOKT:]),
            ):
                total = result[:, HD:]
                level = level * SCALE + jnp.log2(total)
                result = result[:, :HD] / total
                if e % 2 == 0:
                    part[e // 2, tile_kind] = result
                else:
                    p1_send[h, e // 2, tile_kind] = result.astype(jnp.bfloat16)
                levels = jnp.where(feature == tile_kind, level, levels)
            all_levels.append(levels)
        return all_levels

    def after_core(h, n):
        arrived(h, *((P_CORE0, L_CORE0) if n == 0 else (P_CORE1, L_CORE1)))
        mine, theirs = lse[n], l1_recv[h, n]
        newest = jnp.maximum(mine, theirs)
        mine_part, theirs_part = jnp.exp2(mine - newest), jnp.exp2(theirs - newest)
        total = mine_part + theirs_part
        mine_part, theirs_part = mine_part / total, theirs_part / total
        for tile_kind in range(3):
            result = (
                part[n, tile_kind] * mine_part[:, tile_kind : tile_kind + 1]
                + p1_recv[h, n, tile_kind].astype(jnp.float32)
                * theirs_part[:, tile_kind : tile_kind + 1]
            )
            if n == 0:
                if tile_kind == O:
                    keep0[h] = result
                else:
                    p2_send0[h, tile_kind // 2] = result.astype(jnp.bfloat16)
            elif tile_kind == O:
                p2_send1[h] = result.astype(jnp.bfloat16)
            else:
                keep1[h, tile_kind // 2] = result
        start(h, P_CHIP0 if n == 0 else P_CHIP1)
        l2_rows[h, n] = gathered(newest + jnp.log2(total))
        start(h, L_CHIP0 if n == 0 else L_CHIP1)

    def after_chip(h):
        arrived(h, P_CHIP0, L_CHIP0)
        mine, theirs = l2_rows[h, 1], l2_recv[h, 0]
        newest = jnp.maximum(mine, theirs)
        mine_part, theirs_part = jnp.exp2(mine - newest), jnp.exp2(theirs - newest)
        total = mine_part + theirs_part
        l3_rows[h] = newest + jnp.log2(total)
        start(h, L_UP, L_DOWN)
        columns = spread(jnp.concatenate([mine_part / total, theirs_part / total], axis=0))
        for n, (tile_kind, number) in enumerate(((U, P_UP), (D, P_DOWN))):
            result = (
                keep1[h, n] * columns[:, tile_kind : tile_kind + 1]
                + p2_recv0[h, n].astype(jnp.float32) * columns[:, 8 + tile_kind : 9 + tile_kind]
            )
            p3_send[h, n] = result.astype(jnp.bfloat16)
            start(h, number)

    def after_row(h):
        arrived(h, P_CHIP1, L_CHIP1, P_UP, L_UP, P_DOWN, L_DOWN)
        levels = (
            l2_rows[h, 0][O : O + 1],
            l2_recv[h, 1][O : O + 1],
            l3_recv[h, 0][U : U + 1],
            l3_recv[h, 1][D : D + 1],
        )
        newest = functools.reduce(jnp.maximum, levels)
        parts = [jnp.exp2(x - newest) for x in levels]
        total = parts[0] + parts[1] + parts[2] + parts[3]
        columns = spread(
            jnp.concatenate(
                [x / total for x in parts] + [jnp.zeros((4, 256), jnp.float32)], axis=0
            )
        )
        result = (
            keep0[h] * columns[:, 0:1]
            + p2_recv1[h].astype(jnp.float32) * columns[:, 1:2]
            + p3_recv[h, 0].astype(jnp.float32) * columns[:, 2:3]
            + p3_recv[h, 1].astype(jnp.float32) * columns[:, 3:4]
        )
        lanes = pl.ds(pl.multiple_of(h * HD, HD), HD)
        out_ref[0, :, lanes] = result.astype(jnp.bfloat16)

    share(0)
    relay(1)
    ask(3)

    def step(i, carry):
        @pl.when(i < ROUNDS)
        def _():
            arrived(i, Q_CORE0, Q_CORE2, Z_RIGHT0, Z_LEFT0, Z_RIGHT1, Z_LEFT1)
            l1_send[i, 0], l1_send[i, 1] = compute(i, (1, 3))
            start(i, P_CORE0, L_CORE0, P_CORE1, L_CORE1)
            lse[0], lse[1] = compute(i, (0, 2))

            @pl.when(i + 1 < ROUNDS)
            def _():
                share(i + 1)

            @pl.when(i + 2 < ROUNDS)
            def _():
                relay(i + 2)

            @pl.when(i + 4 < ROUNDS)
            def _():
                ask(i + 4)

            after_core(i, 0)
            after_core(i, 1)

        @pl.when(i >= 1)
        def _():
            after_chip(i - 1)

        return carry

    lax.fori_loop(0, ROUNDS + 1, step, 0)

    def result_of(h, carry):
        after_row(h)
        return carry

    lax.fori_loop(0, ROUNDS, result_of, 0)

    def finish(h, carry):
        for number in range(MESSAGES):
            messages[number](h).wait_send()
        return carry

    lax.fori_loop(0, ROUNDS, finish, 0)
    for copy in par_copies:
        copy.wait_send()


def solution(mesh):
    grid_rows = mesh.shape["tile"] // GX
    bf16, f32, i32 = jnp.bfloat16, jnp.float32, jnp.int32
    wide = GROUPS * ROUNDS * HD

    def on_device(queries, keys, values, cache_keys, cache_values, order, tile_mask, reach):
        smem = pl.BlockSpec(memory_space=pltpu.SMEM)
        anywhere = pl.BlockSpec(memory_space=pl.ANY)
        piece = (TOKT, HD)
        return pl.pallas_call(
            functools.partial(kernel, grid_rows),
            out_shape=jax.ShapeDtypeStruct((1, TOKT, ROUNDS * HD), bf16),
            in_specs=[smem] * 3 + [anywhere] * 5,
            out_specs=pl.BlockSpec(memory_space=pltpu.VMEM),
            scratch_shapes=[
                pltpu.VMEM((1, TOKT, ROUNDS * HD), bf16),
                pltpu.VMEM((1, TOKT, ROUNDS * HD), bf16),
                pltpu.VMEM((1, TOKT, ROUNDS * HD), bf16),
                pltpu.VMEM((1, 1, TOKT, wide), bf16),
                pltpu.VMEM((1, 1, TOKT, wide), bf16),
                pltpu.VMEM((ROUNDS, 4, 2, 3, 2, HALF, HD), bf16),
                pltpu.VMEM((ROUNDS, 4, 2, 2, 2, HALF, HD), bf16),
                pltpu.VMEM((ROUNDS, GROUPS, 3) + piece, bf16),
                pltpu.VMEM((16, HD), i32),
                pltpu.VMEM((16, HD), i32),
                pltpu.VMEM((16, HD), i32),
                pltpu.VMEM((2,) + piece, bf16),
                pltpu.VMEM((3, 2) + piece, f32),
                pltpu.VMEM((2, 3) + piece, f32),
                pltpu.VMEM((2,) + piece, f32),
                pltpu.VMEM((ROUNDS, 2, 3) + piece, bf16),
                pltpu.VMEM((ROUNDS, 2, 3) + piece, bf16),
                pltpu.VMEM((ROUNDS, 2) + piece, f32),
                pltpu.VMEM((ROUNDS, 2) + piece, f32),
                pltpu.VMEM((ROUNDS, 2) + piece, bf16),
                pltpu.VMEM((ROUNDS, 2) + piece, bf16),
                pltpu.VMEM((ROUNDS,) + piece, bf16),
                pltpu.VMEM((ROUNDS,) + piece, bf16),
                pltpu.VMEM((ROUNDS,) + piece, f32),
                pltpu.VMEM((ROUNDS, 2) + piece, f32),
                pltpu.VMEM((ROUNDS, 2, 8, 256), f32),
                pltpu.VMEM((ROUNDS, 2, 8, 256), f32),
                pltpu.VMEM((ROUNDS, 2) + piece, bf16),
                pltpu.VMEM((ROUNDS, 2) + piece, bf16),
                pltpu.VMEM((ROUNDS, 8, 256), f32),
                pltpu.VMEM((ROUNDS, 2, 8, 256), f32),
                pltpu.SemaphoreType.DMA((5,)),
                pltpu.SemaphoreType.DMA((2,)),
                pltpu.SemaphoreType.DMA((2,)),
                pltpu.SemaphoreType.DMA((MESSAGES, ROUNDS)),
                pltpu.SemaphoreType.DMA((MESSAGES, ROUNDS)),
            ],
            compiler_params=pltpu.CompilerParams(
                collective_id=0, has_side_effects=True, vmem_limit_bytes=56 * 2**20
            ),
        )(order, tile_mask, reach, queries, keys, values, cache_keys, cache_values)

    placed = (
        P("tile", None, "slot"),
        P("tile", None, "slot"),
        P("tile", None, "slot"),
        P("slot", "tile", None, None),
        P("slot", "tile", None, None),
        P(),
        P("tile", None),
        P("tile", None),
    )
    return jax.shard_map(
        on_device, mesh=mesh, in_specs=placed, out_specs=P("tile", None, "slot"), check_vma=False
    )
```

```python
import functools
import math

import jax
import jax.numpy as jnp
from jax import lax
from jax.experimental import pallas as pl
from jax.experimental.pallas import tpu as pltpu
from jax.sharding import PartitionSpec as P

TH = 8
TW = 8
F = 3
HALO = 4
GX = 8
HD = 128
PAIRS = 22
TOKT = 192
STRETCHES = 4
HALF = 48
ROUNDS = 5
GROUPS = 4
NEGATIVE = -1e30
SCALE = math.log2(math.e) / math.sqrt(HD)
MESH = pl.DeviceIdType.MESH
U, O, D = 0, 1, 2
(
    Z_RIGHT0,
    Z_LEFT0,
    Z_RIGHT1,
    Z_LEFT1,
    Q_CHIP,
    Q_UP,
    Q_UP2,
    Q_DOWN,
    Q_PASS,
    Q_CORE0,
    Q_CORE2,
    P_CORE0,
    L_CORE0,
    P_CORE1,
    L_CORE1,
    P_CHIP0,
    L_CHIP0,
    P_CHIP1,
    L_CHIP1,
    P_UP,
    L_UP,
    P_DOWN,
    L_DOWN,
    MESSAGES,
) = range(24)


def nt_dot(a, b):
    return lax.dot_general(a, b, (((1,), (1,)), ((), ())), preferred_element_type=jnp.float32)


def dot(a, b):
    return lax.dot_general(a, b, (((1,), (0,)), ((), ())), preferred_element_type=jnp.float32)


def iota(shape, dim):
    return lax.broadcasted_iota(jnp.int32, shape, dim)


def spread(rows):
    padded = jnp.concatenate([rows, jnp.zeros((HD - rows.shape[0], 256), jnp.float32)], axis=0)
    return padded.T[:TOKT]


def gathered(columns):
    padded = jnp.concatenate([columns, jnp.zeros((256 - TOKT, HD), jnp.float32)], axis=0)
    return padded.T[:8]


def kernel(
    grid_rows,
    order_ref,
    mask_ref,
    reach_ref,
    q_hbm,
    k_hbm,
    v_hbm,
    ck_hbm,
    cv_hbm,
    out_ref,
    q_in,
    k_in,
    v_in,
    ck_in,
    cv_in,
    kv0,
    kv1,
    q,
    par,
    par_up,
    par_down,
    bias,
    table,
    part,
    lse,
    p1_send,
    p1_recv,
    l1_send,
    l1_recv,
    p2_send0,
    p2_recv0,
    p2_send1,
    p2_recv1,
    keep0,
    keep1,
    l2_rows,
    l2_recv,
    p3_send,
    p3_recv,
    l3_rows,
    l3_recv,
    in_sem,
    par_send_sem,
    par_recv_sem,
    send_sem,
    recv_sem,
):
    tile = lax.axis_index("tile")
    slot = lax.axis_index("slot")
    row, col = tile // GX, lax.rem(tile, GX)
    tiles = grid_rows * GX
    core_slot = slot + 1 - 2 * lax.rem(slot, 2)
    chip_slot = lax.rem(slot + 2, 4)
    right = row * GX + lax.rem(col + 1, GX)
    left = row * GX + lax.rem(col + GX - 1, GX)
    up = lax.rem(tile + tiles - GX, tiles)
    down = lax.rem(tile + GX, tiles)
    core_mate, chip_mate = (tile, core_slot), (tile, chip_slot)
    at_right, at_left = (right, slot), (left, slot)
    at_up, at_down = (up, chip_slot), (down, chip_slot)

    inputs = [
        pltpu.make_async_copy(source, target, in_sem.at[n])
        for n, (source, target) in enumerate(
            ((ck_hbm, ck_in), (cv_hbm, cv_in), (k_hbm, k_in), (v_hbm, v_in), (q_hbm, q_in))
        )
    ]
    for copy in inputs:
        copy.start()

    barrier = pltpu.get_barrier_semaphore()
    partners = (core_mate, chip_mate, at_right, at_left, at_up, at_down)
    for partner in partners:
        pl.semaphore_signal(barrier, inc=1, device_id=partner, device_id_type=MESH)

    def message(number, h, source, target, device):
        return pltpu.make_async_remote_copy(
            src_ref=source,
            dst_ref=target,
            send_sem=send_sem.at[number, h],
            recv_sem=recv_sem.at[number, h],
            device_id=device,
            device_id_type=MESH,
        )

    messages = {
        Z_RIGHT0: lambda h: message(Z_RIGHT0, h, kv0.at[h, 2], kv0.at[h, 0], at_right),
        Z_LEFT0: lambda h: message(Z_LEFT0, h, kv0.at[h, 1], kv0.at[h, 3], at_left),
        Z_RIGHT1: lambda h: message(Z_RIGHT1, h, kv1.at[h, 2], kv1.at[h, 0], at_right),
        Z_LEFT1: lambda h: message(Z_LEFT1, h, kv1.at[h, 1], kv1.at[h, 3], at_left),
        Q_CHIP: lambda h: message(Q_CHIP, h, q.at[h, 0, O], q.at[h, 2, O], chip_mate),
        Q_UP: lambda h: message(Q_UP, h, q.at[h, 0, O], q.at[h, 2, D], at_up),
        Q_UP2: lambda h: message(Q_UP2, h, q.at[h, 2, O], q.at[h, 0, D], at_up),
        Q_DOWN: lambda h: message(Q_DOWN, h, q.at[h, 0, O], q.at[h, 2, U], at_down),
        Q_PASS: lambda h: message(Q_PASS, h, q.at[h, 2, U], q.at[h, 0, U], chip_mate),
        Q_CORE0: lambda h: message(Q_CORE0, h, q.at[h, 0], q.at[h, 1], core_mate),
        Q_CORE2: lambda h: message(Q_CORE2, h, q.at[h, 2], q.at[h, 3], core_mate),
        P_CORE0: lambda h: message(P_CORE0, h, p1_send.at[h, 0], p1_recv.at[h, 0], core_mate),
        L_CORE0: lambda h: message(L_CORE0, h, l1_send.at[h, 0], l1_recv.at[h, 0], core_mate),
        P_CORE1: lambda h: message(P_CORE1, h, p1_send.at[h, 1], p1_recv.at[h, 1], core_mate),
        L_CORE1: lambda h: message(L_CORE1, h, l1_send.at[h, 1], l1_recv.at[h, 1], core_mate),
        P_CHIP0: lambda h: message(P_CHIP0, h, p2_send0.at[h], p2_recv0.at[h], chip_mate),
        L_CHIP0: lambda h: message(L_CHIP0, h, l2_rows.at[h, 0], l2_recv.at[h, 0], chip_mate),
        P_CHIP1: lambda h: message(P_CHIP1, h, p2_send1.at[h], p2_recv1.at[h], chip_mate),
        L_CHIP1: lambda h: message(L_CHIP1, h, l2_rows.at[h, 1], l2_recv.at[h, 1], chip_mate),
        P_UP: lambda h: message(P_UP, h, p3_send.at[h, 0], p3_recv.at[h, 0], at_up),
        L_UP: lambda h: message(L_UP, h, l3_rows.at[h], l3_recv.at[h, 0], at_up),
        P_DOWN: lambda h: message(P_DOWN, h, p3_send.at[h, 1], p3_recv.at[h, 1], at_down),
        L_DOWN: lambda h: message(L_DOWN, h, l3_rows.at[h], l3_recv.at[h, 1], at_down),
    }

    def start(h, *numbers):
        for number in numbers:
            messages[number](h).start()

    def arrived(h, *numbers):
        for number in numbers:
            messages[number](h).wait_recv()

    age = jnp.int32(0)
    for n in range(STRETCHES):
        age = age + jnp.where(slot == n, order_ref[n], 0)
    sub, lane = iota((8, HD), 0), iota((8, HD), 1)
    moment = jnp.where(sub < F, (STRETCHES - 1 - age) * F + sub, STRETCHES * F + sub - F)
    pair = jnp.where(lane < PAIRS, lane, lane - PAIRS).astype(jnp.float32)
    frequency = jnp.exp(pair * (-math.log(10000.0) / PAIRS))
    angle = jnp.where(lane < 2 * PAIRS, moment.astype(jnp.float32) * frequency, 0.0)
    cosine, sine = jnp.cos(angle), jnp.sin(angle)
    for n in range(2):
        for f in range(F):
            for at, values in ((0, cosine), (1, sine)):
                wanted = jnp.broadcast_to(values[n * F + f : n * F + f + 1], (16, HD))
                for quarter in range(4):
                    table[n, at, pl.ds(quarter * HALF + f * 16, 16)] = wanted
                if n == 1:
                    for part_at in range(4):
                        table[2, at, pl.ds(f * 64 + part_at * 16, 16)] = wanted

    first, second = iota((HD, HD), 0), iota((HD, HD), 1)
    exchange = jnp.where(
        (second < PAIRS) & (first == second + PAIRS),
        -1.0,
        jnp.where((second >= PAIRS) & (second < 2 * PAIRS) & (first == second - PAIRS), 1.0, 0.0),
    ).astype(jnp.bfloat16)
    at = iota((TOKT, TOKT), 0)
    side = (at >= 2 * HALF).astype(jnp.int32)
    rest = at - side * 2 * HALF
    lower = (rest >= HALF).astype(jnp.int32)
    rest = rest - lower * HALF
    source = (
        (rest >> 4) * TH * TW + (lower * HALO + ((rest >> 2) & 3)) * TW + side * HALO + (rest & 3)
    )
    quarters = (iota((TOKT, TOKT), 1) == source).astype(jnp.float32).astype(jnp.bfloat16)

    def turned(x, n):
        swapped = dot(x.astype(jnp.bfloat16), exchange)
        return x.astype(jnp.float32) * table[n, 0] + swapped * table[n, 1]

    def group_of(e):
        if e == 0:
            return slot
        if e == 1:
            return core_slot
        if e == 2:
            return chip_slot
        return 3 - slot

    def prepare_block(h, kv, e, keys, values, n):
        both = dot(quarters, jnp.concatenate([keys, values], axis=1))
        new_keys = turned(both[:, :HD], n).astype(jnp.bfloat16)
        new_values = both[:, HD:].astype(jnp.bfloat16)
        for g in range(2):
            for lower_half in range(2):
                at_row = (g * 2 + lower_half) * HALF
                kv[h, 1 + g, 0, e, lower_half] = new_keys[at_row : at_row + HALF]
                kv[h, 1 + g, 1, e, lower_half] = new_values[at_row : at_row + HALF]

    def prepare(h):
        for e in range(GROUPS):
            lanes = pl.ds(pl.multiple_of((group_of(e) * ROUNDS + h) * HD, HD), HD)
            kv = kv0 if e < 2 else kv1
            prepare_block(h, kv, e % 2, ck_in[0, 0, :, lanes], cv_in[0, 0, :, lanes], 0)
        lanes = pl.ds(pl.multiple_of(h * HD, HD), HD)
        prepare_block(h, kv0, 2, k_in[0, :, lanes], v_in[0, :, lanes], 1)
        q[h, 0, O] = turned(q_in[0, :, lanes], 2).astype(jnp.bfloat16)

    entry = iota((16, HD), 0)
    block = jnp.zeros((16, HD), jnp.int32)
    for n in range(9):
        block = jnp.where(entry == n, mask_ref[0, n], block)
    for n in range(2):
        block = jnp.where(entry == 9 + n, reach_ref[0, n], block)
    par[...] = block

    for copy in inputs:
        copy.wait()
    prepare(0)
    pl.semaphore_wait(barrier, len(partners))

    par_copies = [
        pltpu.make_async_remote_copy(
            src_ref=par,
            dst_ref=target,
            send_sem=par_send_sem.at[n],
            recv_sem=par_recv_sem.at[n],
            device_id=device,
            device_id_type=MESH,
        )
        for n, (target, device) in enumerate(((par_up, at_down), (par_down, at_up)))
    ]
    for copy in par_copies:
        copy.start()

    def relay(h):
        arrived(h, Q_CHIP)
        start(h, Q_UP2)
        arrived(h, Q_DOWN)
        start(h, Q_PASS)

    def share(h):
        arrived(h, Q_UP)
        start(h, Q_CORE2)
        arrived(h, Q_PASS, Q_UP2)
        start(h, Q_CORE0)

    def ask(h):
        start(h, Q_CHIP, Q_DOWN, Q_UP)

    start(0, Z_RIGHT0, Z_LEFT0, Z_RIGHT1, Z_LEFT1)
    ask(0)

    def first_sends(h, carry):
        prepare(h)
        start(h, Z_RIGHT0, Z_LEFT0, Z_RIGHT1, Z_LEFT1)

        @pl.when(h == 1)
        def _():
            ask(1)

        return carry

    lax.fori_loop(1, ROUNDS, first_sends, 0)
    relay(0)
    ask(2)

    for copy in par_copies:
        copy.wait_recv()

    key, feature = iota((TOKT, HD), 0), iota((TOKT, HD), 1)
    from_left, from_right = key < HALF, key >= 3 * HALF
    key_row, key_col = (key >> 2) & 3, key & 3

    def window(values, dy, rows_good):
        bits = [values[(dy + 1) * 3 + n : (dy + 1) * 3 + n + 1] for n in range(3)]
        reach_cols = values[10:11]
        middle = jnp.full((1, HD), 1, jnp.int32) if dy == 0 else bits[1]
        on_left = from_left & (key_col >= HALO - reach_cols) & (bits[0] > 0) & (col >= 1)
        on_right = from_right & (key_col < reach_cols) & (bits[2] > 0) & (col < GX - 1)
        inside = (key >= HALF) & (key < 3 * HALF) & (middle > 0)
        good = (on_left | on_right | inside) & rows_good
        return jnp.where(good, 0.0, NEGATIVE)

    above, below, here = par_up[...], par_down[...], par[...]
    own_window = window(here, 0, key >= 0)
    up_window = window(above, 1, (key_row < above[9:10]) & (row >= 1))
    down_window = window(below, -1, (key_row >= HALO - below[9:10]) & (row < grid_rows - 1))
    for n, other in enumerate((up_window, down_window)):
        bias[n] = jnp.where(
            feature == 0, other, jnp.where(feature == 1, own_window, 0.0)
        ).astype(jnp.bfloat16)

    def compute(h, groups):
        other_marker = jnp.where(feature == 0, 1.0, 0.0).astype(jnp.bfloat16)
        own_marker = jnp.where(feature == 1, 1.0, 0.0).astype(jnp.bfloat16)
        ones = jnp.ones((TOKT, HD), jnp.bfloat16)
        nothing = jnp.concatenate(
            [jnp.zeros((64, HD), jnp.bfloat16), jnp.full((64, HD), NEGATIVE, jnp.bfloat16)], axis=1
        )
        markers = (
            jnp.concatenate([other_marker, own_marker], axis=0),
            jnp.concatenate([own_marker, other_marker], axis=0),
        )
        all_levels = []
        for e in groups:
            levels = jnp.zeros((TOKT, HD), jnp.float32)
            kv = kv0 if e < 2 else kv1
            blocks = (e % 2,) if e > 0 else (0, 2)
            scores, highest = [], []
            for half in range(2):
                keys = jnp.concatenate(
                    [
                        jnp.concatenate(
                            [kv[h, :, 0, n, half].reshape(TOKT, HD), bias[half]], axis=1
                        )
                        for n in blocks
                    ]
                    + ([nothing] if len(blocks) == 1 else []),
                    axis=0,
                )
                queries = q[h, e, pl.ds(half, 2)].reshape(2 * TOKT, HD)
                found = nt_dot(jnp.concatenate([queries, markers[half]], axis=1), keys)
                scores.append(found)
                highest.append(jnp.max(found, axis=1, keepdims=True))
            top, bottom = highest
            own = jnp.maximum(top[TOKT:], bottom[:TOKT])
            highest = (
                jnp.concatenate([top[:TOKT], own], axis=0),
                jnp.concatenate([own, bottom[TOKT:]], axis=0),
            )
            summed = []
            for half in range(2):
                weights = jnp.exp2(scores[half] * SCALE - highest[half] * SCALE).astype(jnp.bfloat16)
                values = jnp.concatenate(
                    [
                        jnp.concatenate([kv[h, :, 1, n, half].reshape(TOKT, HD), ones], axis=1)
                        for n in blocks
                    ]
                    + ([jnp.zeros((64, 2 * HD), jnp.bfloat16)] if len(blocks) == 1 else []),
                    axis=0,
                )
                summed.append(dot(weights, values))
            for tile_kind, result, level in (
                (U, summed[0][:TOKT], top[:TOKT]),
                (O, summed[0][TOKT:] + summed[1][:TOKT], own),
                (D, summed[1][TOKT:], bottom[TOKT:]),
            ):
                total = result[:, HD:]
                level = level * SCALE + jnp.log2(total)
                result = result[:, :HD] / total
                if e % 2 == 0:
                    part[e // 2, tile_kind] = result
                else:
                    p1_send[h, e // 2, tile_kind] = result.astype(jnp.bfloat16)
                levels = jnp.where(feature == tile_kind, level, levels)
            all_levels.append(levels)
        return all_levels

    def after_core(h, n):
        arrived(h, *((P_CORE0, L_CORE0) if n == 0 else (P_CORE1, L_CORE1)))
        mine, theirs = lse[n], l1_recv[h, n]
        newest = jnp.maximum(mine, theirs)
        mine_part, theirs_part = jnp.exp2(mine - newest), jnp.exp2(theirs - newest)
        total = mine_part + theirs_part
        mine_part, theirs_part = mine_part / total, theirs_part / total
        for tile_kind in (U, D, O) if n == 0 else (O, U, D):
            result = (
                part[n, tile_kind] * mine_part[:, tile_kind : tile_kind + 1]
                + p1_recv[h, n, tile_kind].astype(jnp.float32)
                * theirs_part[:, tile_kind : tile_kind + 1]
            )
            if n == 0:
                if tile_kind == O:
                    keep0[h] = result
                else:
                    p2_send0[h, tile_kind // 2] = result.astype(jnp.bfloat16)
            elif tile_kind == O:
                p2_send1[h] = result.astype(jnp.bfloat16)
            else:
                keep1[h, tile_kind // 2] = result
            if tile_kind == (D if n == 0 else O):
                start(h, P_CHIP0 if n == 0 else P_CHIP1)
        l2_rows[h, n] = gathered(newest + jnp.log2(total))
        start(h, L_CHIP0 if n == 0 else L_CHIP1)

    def after_chip(h):
        arrived(h, P_CHIP0, L_CHIP0)
        mine, theirs = l2_rows[h, 1], l2_recv[h, 0]
        newest = jnp.maximum(mine, theirs)
        mine_part, theirs_part = jnp.exp2(mine - newest), jnp.exp2(theirs - newest)
        total = mine_part + theirs_part
        l3_rows[h] = newest + jnp.log2(total)
        start(h, L_UP, L_DOWN)
        columns = spread(jnp.concatenate([mine_part / total, theirs_part / total], axis=0))
        for n, (tile_kind, number) in enumerate(((U, P_UP), (D, P_DOWN))):
            result = (
                keep1[h, n] * columns[:, tile_kind : tile_kind + 1]
                + p2_recv0[h, n].astype(jnp.float32) * columns[:, 8 + tile_kind : 9 + tile_kind]
            )
            p3_send[h, n] = result.astype(jnp.bfloat16)
            start(h, number)

    def after_row(h):
        arrived(h, P_CHIP1, L_CHIP1, P_UP, L_UP, P_DOWN, L_DOWN)
        levels = (
            l2_rows[h, 0][O : O + 1],
            l2_recv[h, 1][O : O + 1],
            l3_recv[h, 0][U : U + 1],
            l3_recv[h, 1][D : D + 1],
        )
        newest = functools.reduce(jnp.maximum, levels)
        parts = [jnp.exp2(x - newest) for x in levels]
        total = parts[0] + parts[1] + parts[2] + parts[3]
        columns = spread(
            jnp.concatenate(
                [x / total for x in parts] + [jnp.zeros((4, 256), jnp.float32)], axis=0
            )
        )
        result = (
            keep0[h] * columns[:, 0:1]
            + p2_recv1[h].astype(jnp.float32) * columns[:, 1:2]
            + p3_recv[h, 0].astype(jnp.float32) * columns[:, 2:3]
            + p3_recv[h, 1].astype(jnp.float32) * columns[:, 3:4]
        )
        lanes = pl.ds(pl.multiple_of(h * HD, HD), HD)
        out_ref[0, :, lanes] = result.astype(jnp.bfloat16)

    share(0)
    relay(1)
    ask(3)

    def step(i, carry):
        @pl.when(i < ROUNDS)
        def _():
            arrived(i, Q_CORE0, Q_CORE2, Z_RIGHT0, Z_LEFT0, Z_RIGHT1, Z_LEFT1)
            l1_send[i, 0], l1_send[i, 1] = compute(i, (1, 3))
            start(i, P_CORE0, L_CORE0, P_CORE1, L_CORE1)
            lse[0], lse[1] = compute(i, (0, 2))

            @pl.when(i + 1 < ROUNDS)
            def _():
                share(i + 1)

            @pl.when(i + 2 < ROUNDS)
            def _():
                relay(i + 2)

            @pl.when(i + 4 < ROUNDS)
            def _():
                ask(i + 4)

            after_core(i, 0)
            after_core(i, 1)

        @pl.when(i >= 1)
        def _():
            after_chip(i - 1)

        return carry

    lax.fori_loop(0, ROUNDS + 1, step, 0)

    def result_of(h, carry):
        after_row(h)
        return carry

    lax.fori_loop(0, ROUNDS, result_of, 0)

    def finish(h, carry):
        for number in range(MESSAGES):
            messages[number](h).wait_send()
        return carry

    lax.fori_loop(0, ROUNDS, finish, 0)
    for copy in par_copies:
        copy.wait_send()


def solution(mesh):
    grid_rows = mesh.shape["tile"] // GX
    bf16, f32, i32 = jnp.bfloat16, jnp.float32, jnp.int32
    wide = GROUPS * ROUNDS * HD

    def on_device(queries, keys, values, cache_keys, cache_values, order, tile_mask, reach):
        smem = pl.BlockSpec(memory_space=pltpu.SMEM)
        anywhere = pl.BlockSpec(memory_space=pl.ANY)
        piece = (TOKT, HD)
        return pl.pallas_call(
            functools.partial(kernel, grid_rows),
            out_shape=jax.ShapeDtypeStruct((1, TOKT, ROUNDS * HD), bf16),
            in_specs=[smem] * 3 + [anywhere] * 5,
            out_specs=pl.BlockSpec(memory_space=pltpu.VMEM),
            scratch_shapes=[
                pltpu.VMEM((1, TOKT, ROUNDS * HD), bf16),
                pltpu.VMEM((1, TOKT, ROUNDS * HD), bf16),
                pltpu.VMEM((1, TOKT, ROUNDS * HD), bf16),
                pltpu.VMEM((1, 1, TOKT, wide), bf16),
                pltpu.VMEM((1, 1, TOKT, wide), bf16),
                pltpu.VMEM((ROUNDS, 4, 2, 3, 2, HALF, HD), bf16),
                pltpu.VMEM((ROUNDS, 4, 2, 2, 2, HALF, HD), bf16),
                pltpu.VMEM((ROUNDS, GROUPS, 3) + piece, bf16),
                pltpu.VMEM((16, HD), i32),
                pltpu.VMEM((16, HD), i32),
                pltpu.VMEM((16, HD), i32),
                pltpu.VMEM((2,) + piece, bf16),
                pltpu.VMEM((3, 2) + piece, f32),
                pltpu.VMEM((2, 3) + piece, f32),
                pltpu.VMEM((2,) + piece, f32),
                pltpu.VMEM((ROUNDS, 2, 3) + piece, bf16),
                pltpu.VMEM((ROUNDS, 2, 3) + piece, bf16),
                pltpu.VMEM((ROUNDS, 2) + piece, f32),
                pltpu.VMEM((ROUNDS, 2) + piece, f32),
                pltpu.VMEM((ROUNDS, 2) + piece, bf16),
                pltpu.VMEM((ROUNDS, 2) + piece, bf16),
                pltpu.VMEM((ROUNDS,) + piece, bf16),
                pltpu.VMEM((ROUNDS,) + piece, bf16),
                pltpu.VMEM((ROUNDS,) + piece, f32),
                pltpu.VMEM((ROUNDS, 2) + piece, f32),
                pltpu.VMEM((ROUNDS, 2, 8, 256), f32),
                pltpu.VMEM((ROUNDS, 2, 8, 256), f32),
                pltpu.VMEM((ROUNDS, 2) + piece, bf16),
                pltpu.VMEM((ROUNDS, 2) + piece, bf16),
                pltpu.VMEM((ROUNDS, 8, 256), f32),
                pltpu.VMEM((ROUNDS, 2, 8, 256), f32),
                pltpu.SemaphoreType.DMA((5,)),
                pltpu.SemaphoreType.DMA((2,)),
                pltpu.SemaphoreType.DMA((2,)),
                pltpu.SemaphoreType.DMA((MESSAGES, ROUNDS)),
                pltpu.SemaphoreType.DMA((MESSAGES, ROUNDS)),
            ],
            compiler_params=pltpu.CompilerParams(
                collective_id=0, has_side_effects=True, vmem_limit_bytes=56 * 2**20
            ),
        )(order, tile_mask, reach, queries, keys, values, cache_keys, cache_values)

    placed = (
        P("tile", None, "slot"),
        P("tile", None, "slot"),
        P("tile", None, "slot"),
        P("slot", "tile", None, None),
        P("slot", "tile", None, None),
        P(),
        P("tile", None),
        P("tile", None),
    )
    return jax.shard_map(
        on_device, mesh=mesh, in_specs=placed, out_specs=P("tile", None, "slot"), check_vma=False
    )
```
